128 devices in a mesh: dp: 4 (over x), shard: 32 (over y, z, core).
Axes of the slice: x: 4, y: 4, z: 4, core: 2. Of those that a mesh axis runs over, the one named last changes fastest.
Arguments:
- grads: bfloat16 [4, 192, 512, 512], P('dp', None, 'shard'), may hold values from -0.59765625 to 0.59765625
- owner_table: int32 [4, 48, 1], replicated, may hold values from 0 to 31; in each aligned block of 48 rows (0 to 47, 48 to 95, ..., all dimensions but the last counted through in order) at most 3 rows name the same one
- momentum: float32 [384, 512, 512], P(('dp', 'shard')), may hold values from -1.2 to 1.2
- variance: float32 [384, 512, 512], P(('dp', 'shard')), may hold values from 0.01 to 0.1
- left_factor: bfloat16 [384, 512, 512], P(('dp', 'shard')), may hold values from -6 to 6
- right_factor: bfloat16 [384, 512, 512], P(('dp', 'shard')), may hold values from -6 to 6
- left_basis: bfloat16 [384, 512, 512], P(('dp', 'shard')), may hold values from -0.25 to 0.25
- right_basis: bfloat16 [384, 512, 512], P(('dp', 'shard')), may hold values from -0.25 to 0.25
Outputs:
- update: bfloat16 [192, 512, 512], P('dp', 'shard')
- new_momentum: float32 [384, 512, 512], P(('dp', 'shard'))
- new_variance: float32 [384, 512, 512], P(('dp', 'shard'))
- new_left_factor: bfloat16 [384, 512, 512], P(('dp', 'shard'))
- new_right_factor: bfloat16 [384, 512, 512], P(('dp', 'shard'))
The draws below stay inside these ranges and needn't reach their ends.
Inputs may be any that keep to these rules, and one draw needn't show every extreme that they name: `owner_table`: within the 48 blocks of one group no owner is named by more than 3 blocks, and in some group an owner is named by exactly 3.
All inputs are finite; a program needn't handle non-finite values.
Results may differ from the reference program's by a relative error of at most 0.013.
Values may be sent and summed in bfloat16 or wider, within the bound.
No kernel may reach another device: no remote copies, remote signals or barrier semaphores. Data moves between devices by JAX's collectives and lax.ppermute only.
A program may use at most 128 MiB of HBM per device.

```python
import math
import jax
import jax.numpy as jnp
import numpy as np
from jax import lax

BS = 512
CAP = 3
NBG = 48
NBLK = 192
SLOTS = 384
N_DP = 4
N_SHARD = 32


def block_levels(key, extent, pieces, least, high):
    loudness, own = 1.0, jax.random.fold_in(key, 6)
    for position, shards_of in pieces:
        draws = jnp.exp(jax.random.uniform(jax.random.fold_in(own, position), (shards_of,), jnp.float32, least / len(pieces), high / len(pieces)))
        loudness = loudness * jnp.repeat(draws, extent[position] // shards_of).reshape([-1 if axis == position else 1 for axis in range(len(extent))])
    return loudness


def assign_block(key, own, number, rows, count, top, reach, lean):
    ranking = jax.random.permutation(key, count)
    crowded, usual = load_shares(count, rows * top, reach, lean, True), load_shares(count, rows * top, reach, lean, False)
    places = jnp.arange(count)

    def named(tallies, offset_by):
        used = int((tallies > 0).sum())
        fixed = max(1, used // 4)
        passed = fixed + (places - fixed + offset_by * (used - fixed)) % max(1, count - fixed)
        return jnp.zeros((count,), jnp.int32).at[ranking[jnp.where(places < fixed, places, passed)]].set(jnp.asarray(tallies, jnp.int32))

    tallies = jnp.where(number % 4 == 0, named(crowded, number // 4), named(usual, number - number // 4 - 1))
    mixed = jax.random.permutation(jax.random.fold_in(own, 3), count)
    donor, sink = mixed[0:count // 2 * 2:2], mixed[1:count // 2 * 2:2]
    margin = jnp.minimum(tallies[donor] - 1, reach - tallies[sink]) // 2
    margin = jnp.where((donor == ranking[0]) | (sink == ranking[0]) | (tallies[sink] == 0), 0, jnp.maximum(margin, 0))
    passed = jax.random.randint(jax.random.fold_in(own, 4), (count // 2,), 0, 1 << 20) % (margin + 1)
    tallies = tallies.at[donor].add(-passed).at[sink].add(passed)
    members = jnp.searchsorted(jnp.cumsum(tallies), jnp.arange(rows * top), side="right").astype(jnp.int32)
    grid = members.reshape(top, rows).T
    grid = grid[jax.random.permutation(jax.random.fold_in(own, 1), rows)]
    offset_by = jax.random.randint(jax.random.fold_in(own, 2), (rows, 1), 0, top)
    return jnp.take_along_axis(grid, (jnp.arange(top)[None, :] + offset_by) % top, axis=1)


def load_shares(amount, total, bound, slope, full):
    portions = [(1 << 20) // math.isqrt(standing ** slope) + 1 for standing in range(1, amount + 1)]
    largest = bound if full else min(bound, max(-(-total // amount), total * portions[0] // sum(portions)))
    least = 1 if total - largest >= amount - 1 else 0
    given, surplus = [largest] + [least] * (amount - 1), total - largest - least * (amount - 1)
    while surplus > 0:
        free = [i for i in range(1, amount) if given[i] < largest] or [i for i in range(1, amount) if given[i] < bound]
        mass, budget = sum([portions[i] for i in free]), surplus
        for i in free:
            extra = min(bound - given[i], max(1, budget * portions[i] // mass), surplus)
            given[i] = given[i] + extra
            surplus = surplus - extra
    return np.array(given)


def normal_values(key, shape, width, limit, split=(), kind=jnp.bfloat16):
    result = jax.random.normal(key, shape, jnp.float32) * width
    if len(split) > 0:
        result = block_levels(key, shape, split, -0.22, 0.18) * result
    return jnp.clip(result, min=-limit, max=limit).astype(kind)


def setup_inputs(seed: int = 0) -> dict:
    keys = jax.random.split(jax.random.key(seed), 9)
    grads = normal_values(keys[0], (N_DP, NBLK, BS, BS), 0.1, 0.59765625, ((0, 4), (2, 32)))
    owner_table_keys = jax.random.split(jax.random.fold_in(keys[1], 1), N_DP * NBG // NBG)
    owner_table_turns = jax.random.permutation(jax.random.fold_in(keys[1], 3), N_DP * NBG // NBG)
    owner_table = jax.vmap(lambda own, number: assign_block(jax.random.fold_in(keys[1], 2), own, number, NBG, N_SHARD, 1, CAP, 1))(owner_table_keys, owner_table_turns).reshape((N_DP, NBG, 1))
    momentum = normal_values(keys[2], (SLOTS, BS, BS), 0.2, 1.2, ((0, 128),), jnp.float32)
    variance = jnp.clip(jnp.exp(math.log(0.1) - 2.3025851 * jax.random.uniform(keys[3], (SLOTS, BS, BS), jnp.float32) ** block_levels(keys[3], (SLOTS, BS, BS), ((0, 128),), -0.2, 0.2)), 0.01, 0.1)
    left_factor = normal_values(keys[4], (SLOTS, BS, BS), 1.0, 6.0, ((0, 128),))
    right_factor = normal_values(keys[5], (SLOTS, BS, BS), 1.0, 6.0, ((0, 128),))
    left_basis = normal_values(keys[6], (SLOTS, BS, BS), BS ** -0.5, 0.25, ((0, 128),))
    right_basis = normal_values(keys[7], (SLOTS, BS, BS), BS ** -0.5, 0.25, ((0, 128),))
    return dict(grads=grads, owner_table=owner_table, momentum=momentum, variance=variance, left_factor=left_factor, right_factor=right_factor, left_basis=left_basis, right_basis=right_basis)


beta_moment = 0.95
beta_second = 0.95
beta_factor = 0.95
epsilon = 1e-08

def owner_ranks(owners, owner_count):
    ident = jnp.arange(owner_count, dtype=jnp.int32)
    onehot = (owners[:, None] == ident[None, :]).astype(jnp.int32)
    before = jnp.cumsum(onehot, axis=0) - onehot
    return lax.optimization_barrier(jnp.sum(before * onehot, axis=1)).astype(jnp.int32)

def block_step(grad_block, moment_old, second_old, left_old, right_old, left_side, right_side):
    moment = beta_moment * moment_old + (1.0 - beta_moment) * grad_block.astype(jnp.float32)
    moment_half = moment.astype(jnp.bfloat16)
    turned_grad = jnp.dot(left_side.T, grad_block, preferred_element_type=jnp.float32).astype(jnp.bfloat16)
    turned_moment = jnp.dot(left_side.T, moment_half, preferred_element_type=jnp.float32).astype(jnp.bfloat16)
    rotated = jnp.dot(turned_grad, right_side, preferred_element_type=jnp.float32)
    rotated_moment = jnp.dot(turned_moment, right_side, preferred_element_type=jnp.float32)
    second = beta_second * second_old + (1.0 - beta_second) * rotated * rotated
    direction = (rotated_moment / (jnp.sqrt(second) + epsilon)).astype(jnp.bfloat16)
    back_half = jnp.dot(left_side, direction, preferred_element_type=jnp.float32).astype(jnp.bfloat16)
    update = jnp.dot(back_half, right_side.T, preferred_element_type=jnp.float32).astype(jnp.bfloat16)
    outer_left = jnp.dot(grad_block, grad_block.T, preferred_element_type=jnp.float32)
    outer_right = jnp.dot(grad_block.T, grad_block, preferred_element_type=jnp.float32)
    new_left = (beta_factor * left_old.astype(jnp.float32) + (1.0 - beta_factor) * outer_left).astype(jnp.bfloat16)
    new_right = (beta_factor * right_old.astype(jnp.float32) + (1.0 - beta_factor) * outer_right).astype(jnp.bfloat16)
    return (update, moment, second, new_left, new_right)

def reference(grads, owner_table, momentum, variance, left_factor, right_factor, left_basis, right_basis):
    summed = lax.optimization_barrier(jnp.sum(grads.astype(jnp.float32), axis=0)).astype(jnp.bfloat16)
    owners = owner_table[:, :, 0]
    ranks = jax.vmap(lambda row: owner_ranks(row, N_SHARD))(owners)
    groups = jnp.arange(N_DP, dtype=jnp.int32)[:, None]
    slots = ((groups * N_SHARD + owners) * CAP + ranks).reshape(-1).astype(jnp.int32)

    def one_block(index):
        slot = slots[index]
        return block_step(summed[index], momentum[slot], variance[slot], left_factor[slot], right_factor[slot], left_basis[slot], right_basis[slot])
    update, moments, seconds, lefts, rights = lax.map(one_block, jnp.arange(summed.shape[0], dtype=jnp.int32))
    new_momentum = momentum.at[slots].set(moments)
    new_variance = variance.at[slots].set(seconds)
    new_left = left_factor.at[slots].set(lefts)
    new_right = right_factor.at[slots].set(rights)
    return (update, new_momentum, new_variance, new_left, new_right)
```

```python
import functools

import jax
import jax.numpy as jnp
from jax import lax
from jax.experimental import pallas as pl
from jax.experimental.pallas import tpu as pltpu
from jax.sharding import PartitionSpec as P

beta_moment = 0.95
beta_second = 0.95
beta_factor = 0.95
epsilon = 1e-08

F32 = jnp.float32
BF16 = jnp.bfloat16
VMEM_LIMIT = 40 * 1024 * 1024


def dot_nn(a, b):
    return lax.dot_general(a, b, (((1,), (0,)), ((), ())), preferred_element_type=F32)


def dot_tn(a, b):
    return lax.dot_general(a, b, (((0,), (0,)), ((), ())), preferred_element_type=F32)


def dot_nt(a, b):
    return lax.dot_general(a, b, (((1,), (1,)), ((), ())), preferred_element_type=F32)


def owner_ranks(owners):
    count = owners.shape[0]
    places = jnp.arange(count, dtype=jnp.int32)
    same = (owners[:, None] == owners[None, :]) & (places[None, :] < places[:, None])
    return jnp.sum(same.astype(jnp.int32), axis=1)


def place_kernel(place_ref, group_ref, own_ref, a_ref, b_ref, c_ref, out_ref):
    del group_ref

    def step(j, carry):
        total = own_ref[j].astype(F32) + a_ref[j].astype(F32)
        total = total + (b_ref[j].astype(F32) + c_ref[j].astype(F32))
        out_ref[place_ref[j]] = total.astype(BF16)
        return carry

    lax.fori_loop(0, a_ref.shape[0], step, 0, unroll=4)


def sum_and_place(local, parts, place, group, slots):
    count, rows, width = parts[0].shape
    block = (count, rows, width)
    whole = pl.BlockSpec(block, lambda i, place, group: (0, 0, 0))
    return pl.pallas_call(
        place_kernel,
        out_shape=jax.ShapeDtypeStruct((slots, rows, width), BF16),
        grid_spec=pltpu.PrefetchScalarGridSpec(
            num_scalar_prefetch=2,
            grid=(1,),
            in_specs=[
                pl.BlockSpec(block, lambda i, place, group: (group[0], 0, 0)),
                whole,
                whole,
                whole,
            ],
            out_specs=pl.BlockSpec((slots, rows, width), lambda i, place, group: (0, 0, 0)),
        ),
        compiler_params=pltpu.CompilerParams(vmem_limit_bytes=VMEM_LIMIT),
        cost_estimate=pl.CostEstimate(
            flops=4 * count * rows * width, bytes_accessed=14 * count * rows * width, transcendentals=0
        ),
        name="sum_and_place",
    )(place, group, local, *parts)


def step_kernel(
    load_ref, grad_ref, mom_ref, var_ref, left_ref, right_ref, mom_out, var_out, upd_out
):
    slot = pl.program_id(0)
    live = slot < load_ref[0]
    size = left_ref.shape[1]

    @pl.when(live)
    def _():
        grad = grad_ref[...].reshape(size, size)
        left = left_ref[0]
        right = right_ref[0]
        moment = beta_moment * mom_ref[0] + (1.0 - beta_moment) * grad.astype(F32)
        mom_out[0] = moment
        turned_grad = dot_tn(left, grad).astype(BF16)
        turned_moment = dot_tn(left, moment.astype(BF16)).astype(BF16)
        rotated = dot_nn(turned_grad, right)
        second = beta_second * var_ref[0] + (1.0 - beta_second) * rotated * rotated
        var_out[0] = second
        rotated_moment = dot_nn(turned_moment, right)
        direction = (rotated_moment / (jnp.sqrt(second) + epsilon)).astype(BF16)
        back_half = dot_nn(left, direction).astype(BF16)
        update = dot_nt(back_half, right).astype(BF16)
        upd_out[...] = update.reshape(upd_out.shape)

    @pl.when(jnp.logical_not(live))
    def _():
        mom_out[...] = mom_ref[...]
        var_out[...] = var_ref[...]


def owner_step(load, grad, momentum, variance, left_basis, right_basis):
    slots, size, _ = momentum.shape
    owners, _, rows, _ = grad.shape
    square = pl.BlockSpec((1, size, size), lambda s, load: (s, 0, 0))
    slab = pl.BlockSpec((owners, 1, rows, size), lambda s, load: (0, s, 0, 0))
    return pl.pallas_call(
        step_kernel,
        out_shape=(
            jax.ShapeDtypeStruct(momentum.shape, F32),
            jax.ShapeDtypeStruct(variance.shape, F32),
            jax.ShapeDtypeStruct(grad.shape, BF16),
        ),
        grid_spec=pltpu.PrefetchScalarGridSpec(
            num_scalar_prefetch=1,
            grid=(slots,),
            in_specs=[slab, square, square, square, square],
            out_specs=[square, square, slab],
        ),
        compiler_params=pltpu.CompilerParams(vmem_limit_bytes=VMEM_LIMIT),
        cost_estimate=pl.CostEstimate(
            flops=12 * slots * size**3, bytes_accessed=20 * slots * size**2, transcendentals=slots * size**2
        ),
        name="owner_step",
    )(load, grad, momentum, variance, left_basis, right_basis)


def factor_kernel(load_ref, grad_ref, left_ref, right_ref, left_out, right_out):
    slot = pl.program_id(0)
    live = slot < load_ref[0]
    size = left_ref.shape[1]

    @pl.when(live)
    def _():
        grad = grad_ref[...].reshape(size, size)
        left_out[0] = (
            beta_factor * left_ref[0].astype(F32) + (1.0 - beta_factor) * dot_nt(grad, grad)
        ).astype(BF16)
        right_out[0] = (
            beta_factor * right_ref[0].astype(F32) + (1.0 - beta_factor) * dot_tn(grad, grad)
        ).astype(BF16)

    @pl.when(jnp.logical_not(live))
    def _():
        left_out[...] = left_ref[...]
        right_out[...] = right_ref[...]


def factor_step(load, grad, left_factor, right_factor):
    slots, size, _ = left_factor.shape
    owners, _, rows, _ = grad.shape
    square = pl.BlockSpec((1, size, size), lambda s, load: (s, 0, 0))
    slab = pl.BlockSpec((owners, 1, rows, size), lambda s, load: (0, s, 0, 0))
    return pl.pallas_call(
        factor_kernel,
        out_shape=(
            jax.ShapeDtypeStruct(left_factor.shape, BF16),
            jax.ShapeDtypeStruct(right_factor.shape, BF16),
        ),
        grid_spec=pltpu.PrefetchScalarGridSpec(
            num_scalar_prefetch=1,
            grid=(slots,),
            in_specs=[slab, square, square],
            out_specs=[square, square],
        ),
        compiler_params=pltpu.CompilerParams(vmem_limit_bytes=VMEM_LIMIT),
        cost_estimate=pl.CostEstimate(
            flops=4 * slots * size**3, bytes_accessed=10 * slots * size**2, transcendentals=0
        ),
        name="factor_step",
    )(load, grad, left_factor, right_factor)


def body(
    grads, owner_table, momentum, variance, left_factor, right_factor, left_basis, right_basis
):
    owner_count = lax.axis_size("shard")
    replicas = lax.axis_size("dp")
    group_index = lax.axis_index("dp")
    own_index = lax.axis_index("shard")
    capacity = momentum.shape[0]
    local = grads[0]
    blocks, rows, width = local.shape
    per_group = blocks // replicas

    owners = lax.dynamic_index_in_dim(owner_table[:, :, 0], group_index, 0, keepdims=False)
    place = owners * capacity + owner_ranks(owners)
    load = jnp.sum((owners == own_index).astype(jnp.int32)).reshape(1)

    parts = []
    for hop in (2, 1, 3):
        target = lax.rem(group_index + hop, replicas)
        chunk = lax.dynamic_slice_in_dim(local, target * per_group, per_group, 0)
        parts.append(
            lax.ppermute(chunk, "dp", [(i, (i + hop) % replicas) for i in range(replicas)])
        )
    outgoing = sum_and_place(
        local, parts, place, group_index.reshape(1), owner_count * capacity
    ).reshape(owner_count, capacity, rows, width)
    gathered = lax.all_to_all(outgoing, "shard", split_axis=0, concat_axis=0, tiled=True)
    new_momentum, new_variance, update = owner_step(
        load, gathered, momentum, variance, left_basis, right_basis
    )
    returned = lax.all_to_all(update, "shard", split_axis=0, concat_axis=0, tiled=True)
    new_left, new_right = factor_step(load, gathered, left_factor, right_factor)
    flat = returned.reshape(owner_count * capacity, rows, width)
    update_rows = jnp.take(flat, place, axis=0, mode="clip")
    return (update_rows, new_momentum, new_variance, new_left, new_right)


def solution(mesh):
    state = P(("dp", "shard"), None, None)
    return jax.shard_map(
        body,
        mesh=mesh,
        in_specs=(P("dp", None, "shard", None), P(), state, state, state, state, state, state),
        out_specs=(P("dp", "shard", None), state, state, state, state),
        check_vma=False,
    )
```

```python
import functools

import jax
import jax.numpy as jnp
from jax import lax
from jax.experimental import pallas as pl
from jax.experimental.pallas import tpu as pltpu
from jax.sharding import PartitionSpec as P

beta_moment = 0.95
beta_second = 0.95
beta_factor = 0.95
epsilon = 1e-08

F32 = jnp.float32
BF16 = jnp.bfloat16
VMEM_LIMIT = 32 * 1024 * 1024


def dot_nn(a, b):
    return lax.dot_general(a, b, (((1,), (0,)), ((), ())), preferred_element_type=F32)


def dot_tn(a, b):
    return lax.dot_general(a, b, (((0,), (0,)), ((), ())), preferred_element_type=F32)


def dot_nt(a, b):
    return lax.dot_general(a, b, (((1,), (1,)), ((), ())), preferred_element_type=F32)


def owner_ranks(owners):
    count = owners.shape[0]
    places = jnp.arange(count, dtype=jnp.int32)
    same = (owners[:, None] == owners[None, :]) & (places[None, :] < places[:, None])
    return jnp.sum(same.astype(jnp.int32), axis=1)


ANYWHERE = pl.BlockSpec(memory_space=pl.ANY)
IN_VMEM = pl.BlockSpec(memory_space=pltpu.VMEM)
DMA = pltpu.SemaphoreType.DMA
REPLICAS = 4
CUTS = 2


def call(kernel, name, scalars, operands, outs, scratch, flops, accessed):
    def place(array, where):
        return array if where is pl.ANY else pltpu.with_memory_space_constraint(array, where)

    spaces = [where for _, where in operands]
    spec = lambda where: IN_VMEM if where is pltpu.VMEM else ANYWHERE
    return pl.pallas_call(
        kernel,
        out_shape=[
            pltpu.VMEM(shape, dtype)
            if where is pltpu.VMEM
            else jax.ShapeDtypeStruct(shape, dtype)
            for shape, dtype, where in outs
        ],
        grid_spec=pltpu.PrefetchScalarGridSpec(
            num_scalar_prefetch=len(scalars),
            grid=(1,),
            in_specs=[spec(where) for where in spaces],
            out_specs=[spec(where) for _, _, where in outs],
            scratch_shapes=scratch,
        ),
        compiler_params=pltpu.CompilerParams(vmem_limit_bytes=VMEM_LIMIT),
        cost_estimate=pl.CostEstimate(flops=flops, bytes_accessed=accessed, transcendentals=0),
        name=name,
    )(*scalars, *[place(array, where) for array, where in operands])


def ahead_of(group, hops):
    return lax.rem(group + hops, REPLICAS)


def copy_kernel(halves, group_ref, local_ref, *refs):
    outs, sem = refs[:-1], refs[-1]
    group = group_ref[0]
    count = outs[0].shape[0]
    step = count // CUTS
    reads = []
    for k, (hops, half) in enumerate(halves):
        first = (2 * ahead_of(group, hops) + half) * count
        for i in range(CUTS):
            reads.append(
                pltpu.make_async_copy(
                    local_ref.at[pl.ds(first + i * step, step)],
                    outs[k].at[pl.ds(i * step, step)],
                    sem.at[k, i],
                )
            )
            reads[-1].start()
    for read in reads:
        read.wait()


def copy_halves(local, group, halves, name):
    blocks, rows, width = local.shape
    count = blocks // REPLICAS // 2
    return call(
        functools.partial(copy_kernel, halves),
        name,
        (group,),
        [(local, pltpu.HBM)],
        [((count, rows, width), BF16, pltpu.VMEM)] * len(halves),
        [DMA((len(halves), CUTS))],
        0,
        2 * len(halves) * count * rows * width,
    )


def add_kernel(up_ref, down_ref, a_ref, b_ref, up_out, down_out):
    def step(j, carry):
        up_out[j] = (up_ref[j].astype(F32) + a_ref[j].astype(F32)).astype(BF16)
        down_out[j] = (down_ref[j].astype(F32) + b_ref[j].astype(F32)).astype(BF16)
        return carry

    lax.fori_loop(0, up_ref.shape[0], step, 0, unroll=4)


def add_relayed(own_up, own_down, up, down):
    count, rows, width = up.shape
    return call(
        add_kernel,
        "add_relayed",
        (),
        [(array, pltpu.VMEM) for array in (own_up, own_down, up, down)],
        [((count, rows, width), BF16, pltpu.VMEM)] * 2,
        [],
        2 * count * rows * width,
        12 * count * rows * width,
    )


def place_kernel(place_ref, own_a, own_b, a1, a2, b1, b2, out_ref, held, sem):
    count = a1.shape[0]
    for own, left, right, base in ((own_a, a1, a2, 0), (own_b, b1, b2, count)):

        def step(j, carry, own=own, left=left, right=right, base=base):
            total = own[j].astype(F32) + (left[j].astype(F32) + right[j].astype(F32))
            held[base + j] = total.astype(BF16)
            pltpu.make_async_copy(
                held.at[base + j], out_ref.at[place_ref[base + j]], sem
            ).start()
            return carry

        lax.fori_loop(0, count, step, 0, unroll=4)
    pltpu.make_async_copy(held, held, sem).wait()


def sum_and_place(own, a, b, place, slots):
    count, rows, width = a[0].shape
    return call(
        place_kernel,
        "sum_and_place",
        (place,),
        [(array, pltpu.VMEM) for array in (*own, *a, *b)],
        [((slots, rows, width), BF16, pltpu.HBM)],
        [pltpu.VMEM((2 * count, rows, width), BF16), DMA(())],
        4 * count * rows * width,
        16 * count * rows * width,
    )[0]


def take_kernel(place_ref, source_ref, out_ref, held, into, out_of):
    cuts = into.shape[0]
    part = out_ref.shape[0] // cuts
    for i in range(cuts):

        def step(j, carry, i=i):
            pltpu.make_async_copy(source_ref.at[place_ref[j]], held.at[j], into.at[i]).start()
            return carry

        lax.fori_loop(i * part, (i + 1) * part, step, 0, unroll=4)
    writes = []
    for i in range(cuts):
        rows = pl.ds(i * part, part)
        pltpu.make_async_copy(held.at[rows], held.at[rows], into.at[i]).wait()
        writes.append(pltpu.make_async_copy(held.at[rows], out_ref.at[rows], out_of.at[i]))
        writes[-1].start()
    for write in writes:
        write.wait()


def take_blocks(source, place):
    _, rows, width = source.shape
    count = place.shape[0]
    return call(
        take_kernel,
        "take_blocks",
        (place,),
        [(source, pl.ANY)],
        [((count, rows, width), BF16, pltpu.HBM)],
        [pltpu.VMEM((count, rows, width), BF16), DMA((3,)), DMA((3,))],
        0,
        4 * count * rows * width,
    )[0]


def turn_kernel(
    mom_ref,
    var_ref,
    left_ref,
    right_ref,
    turned_first,
    var_first,
    left_first,
    right_first,
    turned_out,
    mom,
    left,
    right,
    turned,
    into,
    out_of,
):
    slots = mom.shape[0]
    reads = [
        [
            pltpu.make_async_copy(a.at[s], b, into.at[s, k])
            for k, (a, b) in enumerate(
                (
                    (mom_ref, mom.at[s]),
                    (left_ref, left.at[s - 1] if s else left_first),
                    (right_ref, right.at[s - 1] if s else right_first),
                )
            )
        ]
        for s in range(slots)
    ]
    reads[0].append(pltpu.make_async_copy(var_ref.at[0], var_first, into.at[0, 3]))
    writes = [
        pltpu.make_async_copy(turned.at[s], turned_out.at[s], out_of.at[s])
        for s in range(slots - 1)
    ]
    for row in reads:
        for read in row:
            read.start()
    for s in range(slots):
        for read in reads[s]:
            read.wait()
        half = (beta_moment * mom[s]).astype(BF16)
        one, other = (left[s - 1], right[s - 1]) if s else (left_first[...], right_first[...])
        product = dot_nn(dot_tn(one, half).astype(BF16), other)
        if s:
            turned[s - 1] = product
            writes[s - 1].start()
        else:
            turned_first[...] = product
    for write in writes:
        write.wait()


def turn_moment(momentum, variance, left_basis, right_basis):
    slots, size, _ = momentum.shape
    square = (size, size)
    others = (slots - 1, size, size)
    return call(
        turn_kernel,
        "turn_moment",
        (),
        [(array, pltpu.HBM) for array in (momentum, variance, left_basis, right_basis)],
        [
            (square, F32, pltpu.VMEM),
            (square, F32, pltpu.VMEM),
            (square, BF16, pltpu.VMEM),
            (square, BF16, pltpu.VMEM),
            (others, F32, pltpu.HBM),
        ],
        [
            pltpu.VMEM(momentum.shape, F32),
            pltpu.VMEM(others, BF16),
            pltpu.VMEM(others, BF16),
            pltpu.VMEM(others, F32),
            DMA((slots, 4)),
            DMA((slots - 1,)),
        ],
        4 * slots * size**3,
        12 * slots * size**2,
    )


def step_kernel(
    load_ref,
    grad_ref,
    turned_ref,
    var_ref,
    left_ref,
    right_ref,
    turned_first,
    var_first,
    left_first,
    right_first,
    var_out,
    upd_out,
    grad,
    turned,
    var,
    left,
    right,
    kept,
    upd,
    into,
    out_of,
):
    slots, size, _ = kept.shape
    reads = [[pltpu.make_async_copy(grad_ref.at[:, 0], grad.at[0], into.at[0, 0])]]
    for s in range(1, slots):
        pairs = (
            (grad_ref.at[:, s], grad.at[s]),
            (left_ref.at[s], left.at[s - 1]),
            (right_ref.at[s], right.at[s - 1]),
            (var_ref.at[s], var.at[s - 1]),
            (turned_ref.at[s - 1], turned.at[s - 1]),
        )
        reads.append(
            [pltpu.make_async_copy(a, b, into.at[s, k]) for k, (a, b) in enumerate(pairs)]
        )
    writes = [
        (
            pltpu.make_async_copy(kept.at[s], var_out.at[s], out_of.at[s, 0]),
            pltpu.make_async_copy(upd.at[s], upd_out.at[:, s], out_of.at[s, 1]),
        )
        for s in range(slots)
    ]
    for row in reads:
        for read in row:
            read.start()
    for s in range(slots):
        for read in reads[s]:
            read.wait()
        at = (lambda ref, first: ref.at[s - 1]) if s else (lambda ref, first: first)
        old = at(var, var_first)

        @pl.when(s < load_ref[0])
        def _():
            one = at(left, left_first)[...]
            other = at(right, right_first)[...]
            block = grad[s].reshape(size, size)
            rotated = dot_nn(dot_tn(one, block).astype(BF16), other)
            second = beta_second * old[...] + (1.0 - beta_second) * rotated * rotated
            kept[s] = second
            rotated_moment = at(turned, turned_first)[...] + (1.0 - beta_moment) * rotated
            direction = (rotated_moment / (jnp.sqrt(second) + epsilon)).astype(BF16)
            back_half = dot_nn(one, direction).astype(BF16)
            update = dot_nt(back_half, other).astype(BF16)
            upd[s] = update.reshape(upd.shape[1:])

        @pl.when(s >= load_ref[0])
        def _():
            kept[s] = old[...]

        for write in writes[s]:
            write.start()
    for row in writes:
        for write in row:
            write.wait()


def owner_step(load, grad, prepared, variance, left_basis, right_basis):
    slots, size, _ = variance.shape
    owners, _, rows, _ = grad.shape
    slabs = pltpu.VMEM((slots, owners, rows, size), BF16)
    others = (slots - 1, size, size)
    *first, turned = prepared
    return call(
        step_kernel,
        "owner_step",
        (load,),
        [(array, pltpu.HBM) for array in (grad, turned, variance, left_basis, right_basis)]
        + [(array, pltpu.VMEM) for array in first],
        [(variance.shape, F32, pltpu.HBM), (grad.shape, BF16, pltpu.HBM)],
        [
            slabs,
            pltpu.VMEM(others, F32),
            pltpu.VMEM(others, F32),
            pltpu.VMEM(others, BF16),
            pltpu.VMEM(others, BF16),
            pltpu.VMEM(variance.shape, F32),
            slabs,
            DMA((slots, 5)),
            DMA((slots, 2)),
        ],
        8 * slots * size**3,
        8 * slots * size**2,
    )


def state_kernel(
    load_ref,
    grad_ref,
    mom_ref,
    left_ref,
    right_ref,
    mom_out,
    left_out,
    right_out,
    grad,
    mom,
    left,
    right,
    into,
    out_of,
):
    slots, size, _ = mom.shape
    pairs = ((mom_ref, mom), (left_ref, left), (right_ref, right))
    reads = [
        [pltpu.make_async_copy(grad_ref.at[:, s], grad.at[s], into.at[s, 3])]
        + [pltpu.make_async_copy(a.at[s], b.at[s], into.at[s, k]) for k, (a, b) in enumerate(pairs)]
        for s in range(slots)
    ]
    pairs = ((mom, mom_out), (left, left_out), (right, right_out))
    writes = [
        [pltpu.make_async_copy(a.at[s], b.at[s], out_of.at[s, k]) for k, (a, b) in enumerate(pairs)]
        for s in range(slots)
    ]
    for row in reads:
        for read in row:
            read.start()
    for s in range(slots):
        for read in reads[s]:
            read.wait()

        @pl.when(s < load_ref[0])
        def _():
            block = grad[s].reshape(size, size)
            mom[s] = beta_moment * mom[s] + (1.0 - beta_moment) * block.astype(F32)
            outer = dot_nt(block, block)
            left[s] = (beta_factor * left[s].astype(F32) + (1.0 - beta_factor) * outer).astype(BF16)
            outer = dot_tn(block, block)
            right[s] = (beta_factor * right[s].astype(F32) + (1.0 - beta_factor) * outer).astype(
                BF16
            )

        for write in writes[s]:
            write.start()
    for row in writes:
        for write in row:
            write.wait()


def rest_of_state(load, grad, momentum, left_factor, right_factor):
    slots, size, _ = momentum.shape
    owners, _, rows, _ = grad.shape
    shape = momentum.shape
    return call(
        state_kernel,
        "rest_of_state",
        (load,),
        [(array, pltpu.HBM) for array in (grad, momentum, left_factor, right_factor)],
        [(shape, F32, pltpu.HBM), (shape, BF16, pltpu.HBM), (shape, BF16, pltpu.HBM)],
        [
            pltpu.VMEM((slots, owners, rows, size), BF16),
            pltpu.VMEM(shape, F32),
            pltpu.VMEM(shape, BF16),
            pltpu.VMEM(shape, BF16),
            DMA((slots, 4)),
            DMA((slots, 3)),
        ],
        4 * slots * size**3,
        18 * slots * size**2,
    )


def exchange(slabs):
    return lax.all_to_all(slabs, "shard", split_axis=0, concat_axis=0, tiled=True)


def body(
    grads, owner_table, momentum, variance, left_factor, right_factor, left_basis, right_basis
):
    owner_count = lax.axis_size("shard")
    group = lax.axis_index("dp")
    own_index = lax.axis_index("shard")
    capacity = momentum.shape[0]
    local = grads[0]
    _, rows, width = local.shape
    up = lambda x: lax.ppermute(x, "dp", [(i, (i + 1) % REPLICAS) for i in range(REPLICAS)])
    down = lambda x: lax.ppermute(x, "dp", [((i + 1) % REPLICAS, i) for i in range(REPLICAS)])

    here = group.reshape(1)
    relay_up, relay_down, near_up, near_down = copy_halves(
        local, here, ((2, 0), (2, 1), (1, 1), (3, 0)), "copy_sends"
    )
    relay_up, relay_down = up(relay_up), down(relay_down)
    near_up, near_down = up(near_up), down(near_down)
    own_up, own_down, own_a, own_b = copy_halves(
        local, here, ((1, 0), (3, 1), (0, 0), (0, 1)), "copy_own"
    )
    prepared = turn_moment(momentum, variance, left_basis, right_basis)
    relay_up, relay_down, prepared = lax.optimization_barrier((relay_up, relay_down, prepared))
    ahead, behind = add_relayed(own_up, own_down, relay_up, relay_down)
    ahead, behind = up(ahead), down(behind)

    owners = lax.dynamic_index_in_dim(owner_table[:, :, 0], group, 0, keepdims=False)
    place = owners * capacity + owner_ranks(owners)
    load = jnp.sum((owners == own_index).astype(jnp.int32)).reshape(1)

    outgoing = sum_and_place(
        (own_a, own_b), (ahead, near_down), (near_up, behind), place, owner_count * capacity
    ).reshape(owner_count, capacity, rows, width)
    grad = exchange(outgoing)
    new_variance, update = owner_step(load, grad, prepared, variance, left_basis, right_basis)
    returned = exchange(update)
    new_momentum, new_left, new_right = rest_of_state(
        load, grad, momentum, left_factor, right_factor
    )
    update_rows = take_blocks(returned.reshape(owner_count * capacity, rows, width), place)
    return (update_rows, new_momentum, new_variance, new_left, new_right)


def solution(mesh):
    state = P(("dp", "shard"), None, None)
    return jax.shard_map(
        body,
        mesh=mesh,
        in_specs=(P("dp", None, "shard", None), P(), state, state, state, state, state, state),
        out_specs=(P("dp", "shard", None), state, state, state, state),
        check_vma=False,
    )
```

```python
import functools

import jax
import jax.numpy as jnp
from jax import lax
from jax.experimental import pallas as pl
from jax.experimental.pallas import tpu as pltpu
from jax.sharding import PartitionSpec as P

beta_moment = 0.95
beta_second = 0.95
beta_factor = 0.95
epsilon = 1e-08

F32 = jnp.float32
BF16 = jnp.bfloat16
VMEM_LIMIT = 32 * 1024 * 1024


def dot_nn(a, b):
    return lax.dot_general(a, b, (((1,), (0,)), ((), ())), preferred_element_type=F32)


def dot_tn(a, b):
    return lax.dot_general(a, b, (((0,), (0,)), ((), ())), preferred_element_type=F32)


def dot_nt(a, b):
    return lax.dot_general(a, b, (((1,), (1,)), ((), ())), preferred_element_type=F32)


ANYWHERE = pl.BlockSpec(memory_space=pl.ANY)
IN_VMEM = pl.BlockSpec(memory_space=pltpu.VMEM)
IN_SMEM = pl.BlockSpec(memory_space=pltpu.SMEM)
DMA = pltpu.SemaphoreType.DMA
REPLICAS = 4
CUTS = 2


def call(kernel, name, scalars, operands, outs, scratch, flops, accessed):
    def place(array, where):
        free = where in (pl.ANY, pltpu.SMEM)
        return array if free else pltpu.with_memory_space_constraint(array, where)

    spaces = [where for _, where in operands]
    spec = lambda where: {pltpu.VMEM: IN_VMEM, pltpu.SMEM: IN_SMEM}.get(where, ANYWHERE)
    return pl.pallas_call(
        kernel,
        out_shape=[
            jax.ShapeDtypeStruct(shape, dtype) if where is pl.ANY else where(shape, dtype)
            for shape, dtype, where in outs
        ],
        grid_spec=pltpu.PrefetchScalarGridSpec(
            num_scalar_prefetch=len(scalars),
            grid=(1,),
            in_specs=[spec(where) for where in spaces],
            out_specs=[spec(where) for _, _, where in outs],
            scratch_shapes=scratch,
        ),
        compiler_params=pltpu.CompilerParams(vmem_limit_bytes=VMEM_LIMIT),
        cost_estimate=pl.CostEstimate(flops=flops, bytes_accessed=accessed, transcendentals=0),
        name=name,
    )(*scalars, *[place(array, where) for array, where in operands])


def ahead_of(group, hops):
    return lax.rem(group + hops, REPLICAS)


def copy_kernel(halves, group_ref, local_ref, *refs):
    outs, sem = refs[:-1], refs[-1]
    group = group_ref[0]
    count = outs[0].shape[0]
    step = count // CUTS
    reads = []
    for k, (hops, half) in enumerate(halves):
        first = (2 * ahead_of(group, hops) + half) * count
        for i in range(CUTS):
            reads.append(
                pltpu.make_async_copy(
                    local_ref.at[pl.ds(first + i * step, step)],
                    outs[k].at[pl.ds(i * step, step)],
                    sem.at[k, i],
                )
            )
            reads[-1].start()
    for read in reads:
        read.wait()


def copy_halves(local, group, halves, name):
    blocks, rows, width = local.shape
    count = blocks // REPLICAS // 2
    return call(
        functools.partial(copy_kernel, halves),
        name,
        (group,),
        [(local, pltpu.HBM)],
        [((count, rows, width), BF16, pltpu.VMEM)] * len(halves),
        [DMA((len(halves), CUTS))],
        0,
        2 * len(halves) * count * rows * width,
    )


def add_kernel(up_ref, down_ref, a_ref, b_ref, up_out, down_out):
    def step(j, carry):
        up_out[j] = (up_ref[j].astype(F32) + a_ref[j].astype(F32)).astype(BF16)
        down_out[j] = (down_ref[j].astype(F32) + b_ref[j].astype(F32)).astype(BF16)
        return carry

    lax.fori_loop(0, up_ref.shape[0], step, 0, unroll=4)


def add_relayed(own_up, own_down, up, down):
    count, rows, width = up.shape
    return call(
        add_kernel,
        "add_relayed",
        (),
        [(array, pltpu.VMEM) for array in (own_up, own_down, up, down)],
        [((count, rows, width), BF16, pltpu.VMEM)] * 2,
        [],
        2 * count * rows * width,
        12 * count * rows * width,
    )


def place_kernel(place_ref, own_a, own_b, a1, a2, b1, b2, out_ref):
    count = a1.shape[0]
    for own, left, right, base in ((own_a, a1, a2, 0), (own_b, b1, b2, count)):

        def step(j, carry, own=own, left=left, right=right, base=base):
            total = own[j].astype(F32) + (left[j].astype(F32) + right[j].astype(F32))
            out_ref[place_ref[base + j]] = total.astype(BF16)
            return carry

        lax.fori_loop(0, count, step, 0, unroll=4)


def sum_and_place(own, a, b, place, slots):
    count, rows, width = a[0].shape
    return call(
        place_kernel,
        "sum_and_place",
        (place,),
        [(array, pltpu.VMEM) for array in (*own, *a, *b)],
        [((slots, rows, width), BF16, pltpu.VMEM)],
        [],
        4 * count * rows * width,
        16 * count * rows * width,
    )[0]


def take_kernel(place_ref, source_ref, out_ref, sem):
    def step(j, carry):
        pltpu.make_async_copy(source_ref.at[place_ref[j]], out_ref.at[j], sem).start()
        return carry

    lax.fori_loop(0, out_ref.shape[0], step, 0, unroll=4)
    pltpu.make_async_copy(out_ref, out_ref, sem).wait()


def take_blocks(source, place):
    _, rows, width = source.shape
    count = place.shape[0]
    return call(
        take_kernel,
        "take_blocks",
        (place,),
        [(source, pltpu.VMEM)],
        [((count, rows, width), BF16, pltpu.HBM)],
        [DMA(())],
        0,
        4 * count * rows * width,
    )[0]


def turn_kernel(
    here_ref,
    table_ref,
    mom_ref,
    left_ref,
    right_ref,
    place_out,
    load_out,
    left_first,
    right_first,
    turned_first,
    left_second,
    turned_out,
    mom,
    left,
    right,
    turned,
    counts,
    into,
    out_of,
):
    slots = mom.shape[0]
    lefts = [left_first, left_second] + [left.at[s] for s in range(slots - 2)]
    rights = [right_first] + [right.at[s] for s in range(slots - 1)]
    reads = [
        [
            pltpu.make_async_copy(mom_ref.at[s], mom.at[s], into.at[s, 0]),
            pltpu.make_async_copy(left_ref.at[s], lefts[s], into.at[s, 1]),
            pltpu.make_async_copy(right_ref.at[s], rights[s], into.at[s, 2]),
        ]
        for s in range(slots)
    ]
    writes = [
        pltpu.make_async_copy(turned.at[s], turned_out.at[s], out_of.at[s])
        for s in range(slots - 1)
    ]
    for row in reads:
        for read in row:
            read.start()

    owner_count = counts.shape[0]
    group, own_index = here_ref[0], here_ref[1]

    def clear(i, carry):
        counts[i] = 0
        return carry

    def rank(j, carry):
        owner = table_ref[group, j]
        seen = counts[owner]
        counts[owner] = seen + 1
        place_out[j] = owner * slots + seen
        return carry

    lax.fori_loop(0, owner_count, clear, 0)
    lax.fori_loop(0, place_out.shape[0], rank, 0)
    load_out[0] = counts[own_index]

    for s in range(slots):
        for read in reads[s]:
            read.wait()
        half = (beta_moment * mom[s]).astype(BF16)
        product = dot_nn(dot_tn(lefts[s][...], half).astype(BF16), rights[s][...]).astype(BF16)
        if s:
            turned[s - 1] = product
            writes[s - 1].start()
        else:
            turned_first[...] = product
    for write in writes:
        write.wait()


def turn_moment(here, table, owner_count, momentum, left_basis, right_basis):
    slots, size, _ = momentum.shape
    square = (size, size)
    return call(
        turn_kernel,
        "turn_moment",
        (here,),
        [(table, pltpu.SMEM)]
        + [(array, pltpu.HBM) for array in (momentum, left_basis, right_basis)],
        [
            ((table.shape[1],), jnp.int32, pltpu.SMEM),
            ((1,), jnp.int32, pltpu.SMEM),
            (square, BF16, pltpu.VMEM),
            (square, BF16, pltpu.VMEM),
            (square, BF16, pltpu.VMEM),
            (square, BF16, pltpu.VMEM),
            ((slots - 1, size, size), BF16, pltpu.HBM),
        ],
        [
            pltpu.VMEM(momentum.shape, F32),
            pltpu.VMEM((slots - 2, size, size), BF16),
            pltpu.VMEM((slots - 1, size, size), BF16),
            pltpu.VMEM((slots - 1, size, size), BF16),
            pltpu.SMEM((owner_count,), jnp.int32),
            DMA((slots, 3)),
            DMA((slots - 1,)),
        ],
        4 * slots * size**3,
        12 * slots * size**2,
    )


def step_kernel(
    load_ref,
    grad_ref,
    turned_ref,
    var_ref,
    left_ref,
    right_ref,
    left_first,
    right_first,
    turned_first,
    left_second,
    var_out,
    upd_out,
    grad,
    turned,
    var,
    left,
    right,
    kept,
    upd,
    into,
    out_of,
):
    slots, size, _ = kept.shape
    lefts = [left_first, left_second] + [left.at[s] for s in range(slots - 2)]
    rights = [right_first] + [right.at[s] for s in range(slots - 1)]
    turns = [turned_first] + [turned.at[s] for s in range(slots - 1)]
    reads = []
    for s in range(slots):
        pairs = [(grad_ref.at[:, s], grad.at[s])]
        if s >= 2:
            pairs.append((left_ref.at[s], lefts[s]))
        if s >= 1:
            pairs.append((right_ref.at[s], rights[s]))
        early = len(pairs)
        pairs.append((var_ref.at[s], var.at[s]))
        if s >= 1:
            pairs.append((turned_ref.at[s - 1], turns[s]))
        row = [pltpu.make_async_copy(a, b, into.at[s, k]) for k, (a, b) in enumerate(pairs)]
        reads += [row[:early], row[early:]]
    reads.append([])
    writes = [
        [
            pltpu.make_async_copy(upd.at[s], upd_out.at[:, s], out_of.at[s, 0]),
            pltpu.make_async_copy(kept.at[s], var_out.at[s], out_of.at[s, 1]),
        ]
        for s in range(slots)
    ]

    def start(row):
        for read in row:
            read.start()

    def wait(row):
        for read in row:
            read.wait()

    def rotate(s):
        block = grad[s].reshape(size, size)
        return dot_nn(dot_tn(lefts[s][...], block).astype(BF16), rights[s][...])

    def finish(s, rotated):
        second = beta_second * var[s] + (1.0 - beta_second) * rotated * rotated
        rotated_moment = turns[s][...].astype(F32) + (1.0 - beta_moment) * rotated
        direction = (rotated_moment / (jnp.sqrt(second) + epsilon)).astype(BF16)
        back_half = dot_nn(lefts[s][...], direction).astype(BF16)
        update = dot_nt(back_half, rights[s][...]).astype(BF16)
        upd[s] = update.reshape(grad.shape[1:])
        kept[s] = jnp.where(s < load_ref[0], second, var[s])

    for row in reads[:3]:
        start(row)
    wait(reads[0])
    start(reads[3])
    start(reads[4])
    rotated = rotate(0)
    for s in range(slots):
        wait(reads[2 * s + 1])
        wait(reads[2 * s + 2])
        for row in reads[2 * s + 5 : 2 * s + 7]:
            start(row)
        ahead = rotate(s + 1) if s + 1 < slots else None
        finish(s, rotated)
        start(writes[s])
        rotated = ahead
    for row in writes:
        wait(row)


def owner_step(load, grad, turned, variance, left_basis, right_basis, *first):
    slots, size, _ = variance.shape
    owners, _, rows, _ = grad.shape
    return call(
        step_kernel,
        "owner_step",
        (load,),
        [(array, pltpu.HBM) for array in (grad, turned, variance, left_basis, right_basis)]
        + [(array, pltpu.VMEM) for array in first],
        [(variance.shape, F32, pltpu.HBM), (grad.shape, BF16, pltpu.HBM)],
        [
            pltpu.VMEM((slots, owners, rows, size), BF16),
            pltpu.VMEM((slots - 1, size, size), BF16),
            pltpu.VMEM(variance.shape, F32),
            pltpu.VMEM((slots - 2, size, size), BF16),
            pltpu.VMEM((slots - 1, size, size), BF16),
            pltpu.VMEM(variance.shape, F32),
            pltpu.VMEM((slots, owners, rows, size), BF16),
            DMA((slots, 5)),
            DMA((slots, 2)),
        ],
        8 * slots * size**3,
        8 * slots * size**2,
    )


def state_kernel(
    load_ref,
    grad_ref,
    mom_ref,
    left_ref,
    right_ref,
    mom_out,
    left_out,
    right_out,
    grad,
    mom,
    left,
    right,
    into,
    out_of,
):
    slots, size, _ = mom.shape
    pairs = ((mom_ref, mom), (left_ref, left), (right_ref, right))
    reads = [
        [pltpu.make_async_copy(grad_ref.at[:, s], grad.at[s], into.at[s, 3])]
        + [pltpu.make_async_copy(a.at[s], b.at[s], into.at[s, k]) for k, (a, b) in enumerate(pairs)]
        for s in range(slots)
    ]
    pairs = ((mom, mom_out), (left, left_out), (right, right_out))
    writes = [
        [pltpu.make_async_copy(a.at[s], b.at[s], out_of.at[s, k]) for k, (a, b) in enumerate(pairs)]
        for s in range(slots)
    ]
    for row in reads:
        for read in row:
            read.start()
    for s in range(slots):
        for read in reads[s]:
            read.wait()

        @pl.when(s < load_ref[0])
        def _():
            block = grad[s].reshape(size, size)
            mom[s] = beta_moment * mom[s] + (1.0 - beta_moment) * block.astype(F32)
            outer = dot_nt(block, block)
            left[s] = (beta_factor * left[s].astype(F32) + (1.0 - beta_factor) * outer).astype(BF16)
            outer = dot_tn(block, block)
            right[s] = (beta_factor * right[s].astype(F32) + (1.0 - beta_factor) * outer).astype(
                BF16
            )

        for write in writes[s]:
            write.start()
    for row in writes:
        for write in row:
            write.wait()


def rest_of_state(load, grad, momentum, left_factor, right_factor):
    slots, size, _ = momentum.shape
    owners, _, rows, _ = grad.shape
    shape = momentum.shape
    return call(
        state_kernel,
        "rest_of_state",
        (load,),
        [(array, pltpu.HBM) for array in (grad, momentum, left_factor, right_factor)],
        [(shape, F32, pltpu.HBM), (shape, BF16, pltpu.HBM), (shape, BF16, pltpu.HBM)],
        [
            pltpu.VMEM((slots, owners, rows, size), BF16),
            pltpu.VMEM(shape, F32),
            pltpu.VMEM(shape, BF16),
            pltpu.VMEM(shape, BF16),
            DMA((slots, 4)),
            DMA((slots, 3)),
        ],
        4 * slots * size**3,
        18 * slots * size**2,
    )


def exchange(slabs):
    return lax.all_to_all(slabs, "shard", split_axis=0, concat_axis=0, tiled=True)


def body(
    grads, owner_table, momentum, variance, left_factor, right_factor, left_basis, right_basis
):
    owner_count = lax.axis_size("shard")
    group = lax.axis_index("dp")
    own_index = lax.axis_index("shard")
    capacity = momentum.shape[0]
    local = grads[0]
    _, rows, width = local.shape
    up = lambda x: lax.ppermute(x, "dp", [(i, (i + 1) % REPLICAS) for i in range(REPLICAS)])
    down = lambda x: lax.ppermute(x, "dp", [((i + 1) % REPLICAS, i) for i in range(REPLICAS)])

    here = jnp.stack([group, own_index])
    relay_up, relay_down = copy_halves(local, here, ((2, 0), (2, 1)), "copy_relayed")
    relay_up, relay_down = up(relay_up), down(relay_down)
    near_up, near_down, own_up, own_down, own_a, own_b = copy_halves(
        local, here, ((1, 1), (3, 0), (1, 0), (3, 1), (0, 0), (0, 1)), "copy_rest"
    )
    near_up, near_down = up(near_up), down(near_down)
    ahead, behind = add_relayed(own_up, own_down, relay_up, relay_down)
    table = owner_table[:, :, 0]
    ahead, behind, table = lax.optimization_barrier((ahead, behind, table))
    ahead, behind = up(ahead), down(behind)
    place, load, *first, turned = turn_moment(
        here, table, owner_count, momentum, left_basis, right_basis
    )

    outgoing = sum_and_place(
        (own_a, own_b), (ahead, near_down), (near_up, behind), place, owner_count * capacity
    ).reshape(owner_count, capacity, rows, width)
    grad = exchange(outgoing)
    new_variance, update = owner_step(
        load, grad, turned, variance, left_basis, right_basis, *first
    )
    returned = exchange(update)
    new_momentum, new_left, new_right = rest_of_state(
        load, grad, momentum, left_factor, right_factor
    )
    update_rows = take_blocks(returned.reshape(owner_count * capacity, rows, width), place)
    return (update_rows, new_momentum, new_variance, new_left, new_right)


def solution(mesh):
    state = P(("dp", "shard"), None, None)
    return jax.shard_map(
        body,
        mesh=mesh,
        in_specs=(P("dp", None, "shard", None), P(), state, state, state, state, state, state),
        out_specs=(P("dp", "shard", None), state, state, state, state),
        check_vma=False,
    )
```

```python
import functools

import jax
import jax.numpy as jnp
from jax import lax
from jax.experimental import pallas as pl
from jax.experimental.pallas import tpu as pltpu
from jax.sharding import PartitionSpec as P

beta_moment = 0.95
beta_second = 0.95
beta_factor = 0.95
epsilon = 1e-08

F32 = jnp.float32
BF16 = jnp.bfloat16
VMEM_LIMIT = 32 * 1024 * 1024


def dot_nn(a, b):
    return lax.dot_general(a, b, (((1,), (0,)), ((), ())), preferred_element_type=F32)


def dot_tn(a, b):
    return lax.dot_general(a, b, (((0,), (0,)), ((), ())), preferred_element_type=F32)


def dot_nt(a, b):
    return lax.dot_general(a, b, (((1,), (1,)), ((), ())), preferred_element_type=F32)


ANYWHERE = pl.BlockSpec(memory_space=pl.ANY)
IN_VMEM = pl.BlockSpec(memory_space=pltpu.VMEM)
IN_SMEM = pl.BlockSpec(memory_space=pltpu.SMEM)
DMA = pltpu.SemaphoreType.DMA
REPLICAS = 4
CUTS = 2


def call(kernel, name, scalars, operands, outs, scratch, flops, accessed):
    def place(array, where):
        free = where in (pl.ANY, pltpu.SMEM)
        return array if free else pltpu.with_memory_space_constraint(array, where)

    spaces = [where for _, where in operands]
    spec = lambda where: {pltpu.VMEM: IN_VMEM, pltpu.SMEM: IN_SMEM}.get(where, ANYWHERE)
    return pl.pallas_call(
        kernel,
        out_shape=[
            jax.ShapeDtypeStruct(shape, dtype) if where is pl.ANY else where(shape, dtype)
            for shape, dtype, where in outs
        ],
        grid_spec=pltpu.PrefetchScalarGridSpec(
            num_scalar_prefetch=len(scalars),
            grid=(1,),
            in_specs=[spec(where) for where in spaces],
            out_specs=[spec(where) for _, _, where in outs],
            scratch_shapes=scratch,
        ),
        compiler_params=pltpu.CompilerParams(vmem_limit_bytes=VMEM_LIMIT),
        cost_estimate=pl.CostEstimate(flops=flops, bytes_accessed=accessed, transcendentals=0),
        name=name,
    )(*scalars, *[place(array, where) for array, where in operands])


def ahead_of(group, hops):
    return lax.rem(group + hops, REPLICAS)


def copy_kernel(halves, local_ref, *refs):
    outs, sem = refs[:-1], refs[-1]
    group = lax.axis_index("dp")
    count = outs[0].shape[0]
    step = count // CUTS
    reads = []
    for k, (hops, half) in enumerate(halves):
        first = (2 * ahead_of(group, hops) + half) * count
        for i in range(CUTS):
            reads.append(
                pltpu.make_async_copy(
                    local_ref.at[pl.ds(first + i * step, step)],
                    outs[k].at[pl.ds(i * step, step)],
                    sem.at[k, i],
                )
            )
            reads[-1].start()
    for read in reads:
        read.wait()


def copy_halves(local, halves, name):
    blocks, rows, width = local.shape
    count = blocks // REPLICAS // 2
    return call(
        functools.partial(copy_kernel, halves),
        name,
        (),
        [(local, pltpu.HBM)],
        [((count, rows, width), BF16, pltpu.VMEM)] * len(halves),
        [DMA((len(halves), CUTS))],
        0,
        2 * len(halves) * count * rows * width,
    )


def add_kernel(own_ref, got_ref, out_ref):
    def step(j, carry):
        out_ref[j] = (own_ref[j].astype(F32) + got_ref[j].astype(F32)).astype(BF16)
        return carry

    lax.fori_loop(0, own_ref.shape[0], step, 0, unroll=4)


def add_relayed(own, got, name):
    return call(
        add_kernel,
        name,
        (),
        [(own, pltpu.VMEM), (got, pltpu.VMEM)],
        [(own.shape, BF16, pltpu.VMEM)],
        [],
        own.size,
        6 * own.size,
    )[0]


def place_kernel(place_ref, own_a, own_b, a1, a2, b1, b2, out_ref):
    count = a1.shape[0]
    for own, left, right, base in ((own_a, a1, a2, 0), (own_b, b1, b2, count)):

        def step(j, carry, own=own, left=left, right=right, base=base):
            total = own[j].astype(F32) + (left[j].astype(F32) + right[j].astype(F32))
            out_ref[place_ref[base + j]] = total.astype(BF16)
            return carry

        lax.fori_loop(0, count, step, 0, unroll=4)


def sum_and_place(own, a, b, place, slots):
    count, rows, width = a[0].shape
    return call(
        place_kernel,
        "sum_and_place",
        (place,),
        [(array, pltpu.VMEM) for array in (*own, *a, *b)],
        [((slots, rows, width), BF16, pltpu.VMEM)],
        [],
        4 * count * rows * width,
        16 * count * rows * width,
    )[0]


def take_kernel(place_ref, source_ref, out_ref, sem):
    def step(j, carry):
        pltpu.make_async_copy(source_ref.at[place_ref[j]], out_ref.at[j], sem).start()
        return carry

    lax.fori_loop(0, out_ref.shape[0], step, 0, unroll=4)
    pltpu.make_async_copy(out_ref, out_ref, sem).wait()


def take_blocks(source, place):
    _, rows, width = source.shape
    count = place.shape[0]
    return call(
        take_kernel,
        "take_blocks",
        (place,),
        [(source, pltpu.VMEM)],
        [((count, rows, width), BF16, pltpu.HBM)],
        [DMA(())],
        0,
        4 * count * rows * width,
    )[0]


def turn_kernel(
    table_ref,
    mom_ref,
    left_ref,
    right_ref,
    place_out,
    load_out,
    left_first,
    right_first,
    turned_first,
    left_second,
    turned_out,
    mom,
    left,
    right,
    turned,
    counts,
    into,
    out_of,
):
    slots = mom.shape[0]
    lefts = [left_first, left_second] + [left.at[s] for s in range(slots - 2)]
    rights = [right_first] + [right.at[s] for s in range(slots - 1)]
    reads = [
        [
            pltpu.make_async_copy(mom_ref.at[s], mom.at[s], into.at[s, 0]),
            pltpu.make_async_copy(left_ref.at[s], lefts[s], into.at[s, 1]),
            pltpu.make_async_copy(right_ref.at[s], rights[s], into.at[s, 2]),
        ]
        for s in range(slots)
    ]
    writes = [
        pltpu.make_async_copy(turned.at[s], turned_out.at[s], out_of.at[s])
        for s in range(slots - 1)
    ]
    for row in reads:
        for read in row:
            read.start()

    owner_count = counts.shape[0]
    group, own_index = lax.axis_index("dp"), lax.axis_index("shard")

    def clear(i, carry):
        counts[i] = 0
        return carry

    def rank(j, carry):
        owner = table_ref[group, j]
        seen = counts[owner]
        counts[owner] = seen + 1
        place_out[j] = owner * slots + seen
        return carry

    lax.fori_loop(0, owner_count, clear, 0)
    lax.fori_loop(0, place_out.shape[0], rank, 0)
    load_out[0] = counts[own_index]

    for s in range(slots):
        for read in reads[s]:
            read.wait()
        half = (beta_moment * mom[s]).astype(BF16)
        product = dot_nn(dot_tn(lefts[s][...], half).astype(BF16), rights[s][...]).astype(BF16)
        if s:
            turned[s - 1] = product
            writes[s - 1].start()
        else:
            turned_first[...] = product
    for write in writes:
        write.wait()


def turn_moment(table, owner_count, momentum, left_basis, right_basis):
    slots, size, _ = momentum.shape
    square = (size, size)
    return call(
        turn_kernel,
        "turn_moment",
        (),
        [(table, pltpu.SMEM)]
        + [(array, pltpu.HBM) for array in (momentum, left_basis, right_basis)],
        [
            ((table.shape[1],), jnp.int32, pltpu.SMEM),
            ((1,), jnp.int32, pltpu.SMEM),
            (square, BF16, pltpu.VMEM),
            (square, BF16, pltpu.VMEM),
            (square, BF16, pltpu.VMEM),
            (square, BF16, pltpu.VMEM),
            ((slots - 1, size, size), BF16, pltpu.HBM),
        ],
        [
            pltpu.VMEM(momentum.shape, F32),
            pltpu.VMEM((slots - 2, size, size), BF16),
            pltpu.VMEM((slots - 1, size, size), BF16),
            pltpu.VMEM((slots - 1, size, size), BF16),
            pltpu.SMEM((owner_count,), jnp.int32),
            DMA((slots, 3)),
            DMA((slots - 1,)),
        ],
        4 * slots * size**3,
        12 * slots * size**2,
    )


def step_kernel(
    load_ref,
    grad_ref,
    turned_ref,
    var_ref,
    left_ref,
    right_ref,
    left_first,
    right_first,
    turned_first,
    left_second,
    var_out,
    upd_out,
    grad,
    turned,
    var,
    left,
    right,
    kept,
    upd,
    into,
    out_of,
):
    slots, size, _ = kept.shape
    lefts = [left_first, left_second] + [left.at[s] for s in range(slots - 2)]
    rights = [right_first] + [right.at[s] for s in range(slots - 1)]
    turns = [turned_first] + [turned.at[s] for s in range(slots - 1)]
    reads = []
    for s in range(slots):
        pairs = [(grad_ref.at[:, s], grad.at[s])]
        if s >= 2:
            pairs.append((left_ref.at[s], lefts[s]))
        if s >= 1:
            pairs.append((right_ref.at[s], rights[s]))
        early = len(pairs)
        pairs.append((var_ref.at[s], var.at[s]))
        if s >= 1:
            pairs.append((turned_ref.at[s - 1], turns[s]))
        row = [pltpu.make_async_copy(a, b, into.at[s, k]) for k, (a, b) in enumerate(pairs)]
        reads += [row[:early], row[early:]]
    reads.append([])
    writes = [
        [
            pltpu.make_async_copy(upd.at[s], upd_out.at[:, s], out_of.at[s, 0]),
            pltpu.make_async_copy(kept.at[s], var_out.at[s], out_of.at[s, 1]),
        ]
        for s in range(slots)
    ]

    def wait(row):
        for read in row:
            read.wait()

    def rotate(s):
        block = grad[s].reshape(size, size)
        return dot_nn(dot_tn(lefts[s][...], block).astype(BF16), rights[s][...])

    def finish(s, rotated):
        second = beta_second * var[s] + (1.0 - beta_second) * rotated * rotated
        kept[s] = jnp.where(s < load_ref[0], second, var[s])
        writes[s][1].start()
        rotated_moment = turns[s][...].astype(F32) + (1.0 - beta_moment) * rotated
        direction = (rotated_moment / (jnp.sqrt(second) + epsilon)).astype(BF16)
        back_half = dot_nn(lefts[s][...], direction).astype(BF16)
        update = dot_nt(back_half, rights[s][...]).astype(BF16)
        upd[s] = update.reshape(grad.shape[1:])
        writes[s][0].start()

    for row in reads:
        for read in row:
            read.start()
    wait(reads[0])
    rotated = rotate(0)
    for s in range(slots):
        wait(reads[2 * s + 1])
        wait(reads[2 * s + 2])
        ahead = rotate(s + 1) if s + 1 < slots else None
        finish(s, rotated)
        rotated = ahead
    for row in writes:
        wait(row)


def owner_step(load, grad, turned, variance, left_basis, right_basis, *first):
    slots, size, _ = variance.shape
    owners, _, rows, _ = grad.shape
    return call(
        step_kernel,
        "owner_step",
        (load,),
        [(array, pltpu.HBM) for array in (grad, turned, variance, left_basis, right_basis)]
        + [(array, pltpu.VMEM) for array in first],
        [(variance.shape, F32, pltpu.HBM), (grad.shape, BF16, pltpu.HBM)],
        [
            pltpu.VMEM((slots, owners, rows, size), BF16),
            pltpu.VMEM((slots - 1, size, size), BF16),
            pltpu.VMEM(variance.shape, F32),
            pltpu.VMEM((slots - 2, size, size), BF16),
            pltpu.VMEM((slots - 1, size, size), BF16),
            pltpu.VMEM(variance.shape, F32),
            pltpu.VMEM((slots, owners, rows, size), BF16),
            DMA((slots, 5)),
            DMA((slots, 2)),
        ],
        8 * slots * size**3,
        8 * slots * size**2,
    )


def state_kernel(
    load_ref,
    grad_ref,
    mom_ref,
    left_ref,
    right_ref,
    mom_out,
    left_out,
    right_out,
    grad,
    mom,
    left,
    right,
    into,
    out_of,
):
    slots, size, _ = mom.shape
    pairs = ((mom_ref, mom), (left_ref, left), (right_ref, right))
    reads = [
        [pltpu.make_async_copy(grad_ref.at[:, s], grad.at[s], into.at[s, 3])]
        + [pltpu.make_async_copy(a.at[s], b.at[s], into.at[s, k]) for k, (a, b) in enumerate(pairs)]
        for s in range(slots)
    ]
    pairs = ((mom, mom_out), (left, left_out), (right, right_out))
    writes = [
        [pltpu.make_async_copy(a.at[s], b.at[s], out_of.at[s, k]) for k, (a, b) in enumerate(pairs)]
        for s in range(slots)
    ]
    for row in reads:
        for read in row:
            read.start()
    for s in range(slots):
        for read in reads[s]:
            read.wait()

        @pl.when(s < load_ref[0])
        def _():
            block = grad[s].reshape(size, size)
            mom[s] = beta_moment * mom[s] + (1.0 - beta_moment) * block.astype(F32)
            outer = dot_nt(block, block)
            left[s] = (beta_factor * left[s].astype(F32) + (1.0 - beta_factor) * outer).astype(BF16)
            outer = dot_tn(block, block)
            right[s] = (beta_factor * right[s].astype(F32) + (1.0 - beta_factor) * outer).astype(
                BF16
            )

        for write in writes[s]:
            write.start()
    for row in writes:
        for write in row:
            write.wait()


def rest_of_state(load, grad, momentum, left_factor, right_factor):
    slots, size, _ = momentum.shape
    owners, _, rows, _ = grad.shape
    shape = momentum.shape
    return call(
        state_kernel,
        "rest_of_state",
        (load,),
        [(array, pltpu.HBM) for array in (grad, momentum, left_factor, right_factor)],
        [(shape, F32, pltpu.HBM), (shape, BF16, pltpu.HBM), (shape, BF16, pltpu.HBM)],
        [
            pltpu.VMEM((slots, owners, rows, size), BF16),
            pltpu.VMEM(shape, F32),
            pltpu.VMEM(shape, BF16),
            pltpu.VMEM(shape, BF16),
            DMA((slots, 4)),
            DMA((slots, 3)),
        ],
        4 * slots * size**3,
        18 * slots * size**2,
    )


def exchange(slabs):
    return lax.all_to_all(slabs, "shard", split_axis=0, concat_axis=0, tiled=True)


def body(
    grads, owner_table, momentum, variance, left_factor, right_factor, left_basis, right_basis
):
    owner_count = lax.axis_size("shard")
    capacity = momentum.shape[0]
    local = grads[0]
    _, rows, width = local.shape
    up = lambda x: lax.ppermute(x, "dp", [(i, (i + 1) % REPLICAS) for i in range(REPLICAS)])
    down = lambda x: lax.ppermute(x, "dp", [((i + 1) % REPLICAS, i) for i in range(REPLICAS)])

    relay_up, relay_down = copy_halves(local, ((2, 0), (2, 1)), "copy_relayed")
    relay_up, relay_down = up(relay_up), down(relay_down)
    near_up, near_down, own_up, own_down, own_a, own_b = copy_halves(
        local, ((1, 1), (3, 0), (1, 0), (3, 1), (0, 0), (0, 1)), "copy_rest"
    )
    near_up, near_down = up(near_up), down(near_down)
    ahead = add_relayed(own_up, relay_up, "add_up")
    behind = add_relayed(own_down, relay_down, "add_down")
    table = owner_table[:, :, 0]
    ahead, behind, table = lax.optimization_barrier((ahead, behind, table))
    ahead, behind = up(ahead), down(behind)
    place, load, *first, turned = turn_moment(
        table, owner_count, momentum, left_basis, right_basis
    )

    outgoing = sum_and_place(
        (own_a, own_b), (ahead, near_down), (near_up, behind), place, owner_count * capacity
    ).reshape(owner_count, capacity, rows, width)
    grad = exchange(outgoing)
    new_variance, update = owner_step(
        load, grad, turned, variance, left_basis, right_basis, *first
    )
    returned = exchange(update)
    new_momentum, new_left, new_right = rest_of_state(
        load, grad, momentum, left_factor, right_factor
    )
    update_rows = take_blocks(returned.reshape(owner_count * capacity, rows, width), place)
    return (update_rows, new_momentum, new_variance, new_left, new_right)


def solution(mesh):
    state = P(("dp", "shard"), None, None)
    return jax.shard_map(
        body,
        mesh=mesh,
        in_specs=(P("dp", None, "shard", None), P(), state, state, state, state, state, state),
        out_specs=(P("dp", "shard", None), state, state, state, state),
        check_vma=False,
    )
```

```python
import functools

import jax
import jax.numpy as jnp
from jax import lax
from jax.experimental import pallas as pl
from jax.experimental.pallas import tpu as pltpu
from jax.sharding import PartitionSpec as P

beta_moment = 0.95
beta_second = 0.95
beta_factor = 0.95
epsilon = 1e-08

F32 = jnp.float32
BF16 = jnp.bfloat16
VMEM_LIMIT = 32 * 1024 * 1024


def dot_nn(a, b):
    return lax.dot_general(a, b, (((1,), (0,)), ((), ())), preferred_element_type=F32)


def dot_tn(a, b):
    return lax.dot_general(a, b, (((0,), (0,)), ((), ())), preferred_element_type=F32)


def dot_nt(a, b):
    return lax.dot_general(a, b, (((1,), (1,)), ((), ())), preferred_element_type=F32)


ANYWHERE = pl.BlockSpec(memory_space=pl.ANY)
IN_VMEM = pl.BlockSpec(memory_space=pltpu.VMEM)
IN_SMEM = pl.BlockSpec(memory_space=pltpu.SMEM)
DMA = pltpu.SemaphoreType.DMA
REPLICAS = 4
CUTS = 2


def call(kernel, name, scalars, operands, outs, scratch, flops, accessed):
    def place(array, where):
        free = where in (pl.ANY, pltpu.SMEM)
        return array if free else pltpu.with_memory_space_constraint(array, where)

    spaces = [where for _, where in operands]
    spec = lambda where: {pltpu.VMEM: IN_VMEM, pltpu.SMEM: IN_SMEM}.get(where, ANYWHERE)
    return pl.pallas_call(
        kernel,
        out_shape=[
            jax.ShapeDtypeStruct(shape, dtype) if where is pl.ANY else where(shape, dtype)
            for shape, dtype, where in outs
        ],
        grid_spec=pltpu.PrefetchScalarGridSpec(
            num_scalar_prefetch=len(scalars),
            grid=(1,),
            in_specs=[spec(where) for where in spaces],
            out_specs=[spec(where) for _, _, where in outs],
            scratch_shapes=scratch,
        ),
        compiler_params=pltpu.CompilerParams(vmem_limit_bytes=VMEM_LIMIT),
        cost_estimate=pl.CostEstimate(flops=flops, bytes_accessed=accessed, transcendentals=0),
        name=name,
    )(*scalars, *[place(array, where) for array, where in operands])


def ahead_of(group, hops):
    return lax.rem(group + hops, REPLICAS)


def copy_kernel(halves, local_ref, *refs):
    outs, sem = refs[:-1], refs[-1]
    group = lax.axis_index("dp")
    count = outs[0].shape[0]
    step = count // CUTS
    reads = []
    for k, (hops, half) in enumerate(halves):
        first = (2 * ahead_of(group, hops) + half) * count
        for i in range(CUTS):
            reads.append(
                pltpu.make_async_copy(
                    local_ref.at[pl.ds(first + i * step, step)],
                    outs[k].at[pl.ds(i * step, step)],
                    sem.at[k, i],
                )
            )
            reads[-1].start()
    for read in reads:
        read.wait()


def copy_halves(local, halves, name):
    blocks, rows, width = local.shape
    count = blocks // REPLICAS // 2
    return call(
        functools.partial(copy_kernel, halves),
        name,
        (),
        [(local, pltpu.HBM)],
        [((count, rows, width), BF16, pltpu.VMEM)] * len(halves),
        [DMA((len(halves), CUTS))],
        0,
        2 * len(halves) * count * rows * width,
    )


def add_kernel(own_ref, got_ref, out_ref):
    def step(j, carry):
        out_ref[j] = (own_ref[j].astype(F32) + got_ref[j].astype(F32)).astype(BF16)
        return carry

    lax.fori_loop(0, own_ref.shape[0], step, 0, unroll=4)


def add_relayed(own, got, name):
    return call(
        add_kernel,
        name,
        (),
        [(own, pltpu.VMEM), (got, pltpu.VMEM)],
        [(own.shape, BF16, pltpu.VMEM)],
        [],
        own.size,
        6 * own.size,
    )[0]


def place_kernel(place_ref, own_a, own_b, a1, a2, b1, b2, out_ref):
    count = a1.shape[0]
    for own, left, right, base in ((own_a, a1, a2, 0), (own_b, b1, b2, count)):

        def step(j, carry, own=own, left=left, right=right, base=base):
            total = own[j].astype(F32) + (left[j].astype(F32) + right[j].astype(F32))
            out_ref[place_ref[base + j]] = total.astype(BF16)
            return carry

        lax.fori_loop(0, count, step, 0, unroll=4)


def sum_and_place(own, a, b, place, slots):
    count, rows, width = a[0].shape
    return call(
        place_kernel,
        "sum_and_place",
        (place,),
        [(array, pltpu.VMEM) for array in (*own, *a, *b)],
        [((slots, rows, width), BF16, pltpu.VMEM)],
        [],
        4 * count * rows * width,
        16 * count * rows * width,
    )[0]


def take_kernel(place_ref, source_ref, out_ref, sem):
    def step(j, carry):
        pltpu.make_async_copy(source_ref.at[place_ref[j]], out_ref.at[j], sem).start()
        return carry

    lax.fori_loop(0, out_ref.shape[0], step, 0, unroll=4)
    pltpu.make_async_copy(out_ref, out_ref, sem).wait()


def take_blocks(source, place):
    _, rows, width = source.shape
    count = place.shape[0]
    return call(
        take_kernel,
        "take_blocks",
        (place,),
        [(source, pltpu.VMEM)],
        [((count, rows, width), BF16, pltpu.HBM)],
        [DMA(())],
        0,
        4 * count * rows * width,
    )[0]


def turn_kernel(
    table_ref,
    mom_ref,
    var_ref,
    left_ref,
    right_ref,
    place_out,
    load_out,
    turned,
    var,
    left,
    right,
    mom,
    counts,
    into,
):
    slots = mom.shape[0]
    pairs = ((mom_ref, mom), (left_ref, left), (right_ref, right), (var_ref, var))
    reads = [
        [pltpu.make_async_copy(a.at[s], b.at[s], into.at[s, k]) for k, (a, b) in enumerate(pairs)]
        for s in range(slots)
    ]
    for row in reads:
        for read in row:
            read.start()

    owner_count = counts.shape[0]
    group, own_index = lax.axis_index("dp"), lax.axis_index("shard")

    def clear(i, carry):
        counts[i] = 0
        return carry

    def rank(j, carry):
        owner = table_ref[group, j]
        seen = counts[owner]
        counts[owner] = seen + 1
        place_out[j] = owner * slots + seen
        return carry

    lax.fori_loop(0, owner_count, clear, 0)
    lax.fori_loop(0, place_out.shape[0], rank, 0)
    load_out[0] = counts[own_index]

    for s in range(slots):
        for read in reads[s]:
            read.wait()
        half = (beta_moment * mom[s]).astype(BF16)
        turned[s] = dot_nn(dot_tn(left[s], half).astype(BF16), right[s])


def turn_moment(table, owner_count, momentum, variance, left_basis, right_basis):
    slots, size, _ = momentum.shape
    shape = momentum.shape
    return call(
        turn_kernel,
        "turn_moment",
        (),
        [(table, pltpu.SMEM)]
        + [(array, pltpu.HBM) for array in (momentum, variance, left_basis, right_basis)],
        [
            ((table.shape[1],), jnp.int32, pltpu.SMEM),
            ((1,), jnp.int32, pltpu.SMEM),
            (shape, F32, pltpu.VMEM),
            (shape, F32, pltpu.VMEM),
            (shape, BF16, pltpu.VMEM),
            (shape, BF16, pltpu.VMEM),
        ],
        [
            pltpu.VMEM(shape, F32),
            pltpu.SMEM((owner_count,), jnp.int32),
            DMA((slots, 4)),
        ],
        4 * slots * size**3,
        12 * slots * size**2,
    )


def step_kernel(
    load_ref, grad, turned, var, left, right, var_out, upd_out, kept, upd, out_of
):
    slots, size, _ = kept.shape
    writes = [
        [
            pltpu.make_async_copy(upd.at[s], upd_out.at[:, s], out_of.at[s, 0]),
            pltpu.make_async_copy(kept.at[s], var_out.at[s], out_of.at[s, 1]),
        ]
        for s in range(slots)
    ]

    def rotate(s):
        block = grad[:, s].reshape(size, size)
        return dot_nn(dot_tn(left[s], block).astype(BF16), right[s])

    def finish(s, rotated):
        second = beta_second * var[s] + (1.0 - beta_second) * rotated * rotated
        kept[s] = jnp.where(s < load_ref[0], second, var[s])
        writes[s][1].start()
        rotated_moment = turned[s] + (1.0 - beta_moment) * rotated
        direction = (rotated_moment / (jnp.sqrt(second) + epsilon)).astype(BF16)
        back_half = dot_nn(left[s], direction).astype(BF16)
        update = dot_nt(back_half, right[s]).astype(BF16)
        upd[s] = update.reshape(upd.shape[1:])
        writes[s][0].start()

    rotated = rotate(0)
    for s in range(slots):
        ahead = rotate(s + 1) if s + 1 < slots else None
        finish(s, rotated)
        rotated = ahead
    for row in writes:
        for write in row:
            write.wait()


def owner_step(load, grad, turned, variance, left_basis, right_basis):
    slots, size, _ = variance.shape
    owners, _, rows, _ = grad.shape
    slabs = pltpu.VMEM((slots, owners, rows, size), BF16)
    return call(
        step_kernel,
        "owner_step",
        (load,),
        [(array, pltpu.VMEM) for array in (grad, turned, variance, left_basis, right_basis)],
        [(variance.shape, F32, pltpu.HBM), (grad.shape, BF16, pltpu.HBM)],
        [pltpu.VMEM(variance.shape, F32), slabs, DMA((slots, 2))],
        8 * slots * size**3,
        8 * slots * size**2,
    )


def state_kernel(
    load_ref,
    grad_ref,
    mom_ref,
    left_ref,
    right_ref,
    mom_out,
    left_out,
    right_out,
    grad,
    mom,
    left,
    right,
    into,
    out_of,
):
    slots, size, _ = mom.shape
    pairs = ((mom_ref, mom), (left_ref, left), (right_ref, right))
    reads = [
        [pltpu.make_async_copy(grad_ref.at[:, s], grad.at[s], into.at[s, 3])]
        + [pltpu.make_async_copy(a.at[s], b.at[s], into.at[s, k]) for k, (a, b) in enumerate(pairs)]
        for s in range(slots)
    ]
    pairs = ((mom, mom_out), (left, left_out), (right, right_out))
    writes = [
        [pltpu.make_async_copy(a.at[s], b.at[s], out_of.at[s, k]) for k, (a, b) in enumerate(pairs)]
        for s in range(slots)
    ]
    for row in reads:
        for read in row:
            read.start()
    for s in range(slots):
        for read in reads[s]:
            read.wait()

        @pl.when(s < load_ref[0])
        def _():
            block = grad[s].reshape(size, size)
            mom[s] = beta_moment * mom[s] + (1.0 - beta_moment) * block.astype(F32)
            outer = dot_nt(block, block)
            left[s] = (beta_factor * left[s].astype(F32) + (1.0 - beta_factor) * outer).astype(BF16)
            outer = dot_tn(block, block)
            right[s] = (beta_factor * right[s].astype(F32) + (1.0 - beta_factor) * outer).astype(
                BF16
            )

        for write in writes[s]:
            write.start()
    for row in writes:
        for write in row:
            write.wait()


def rest_of_state(load, grad, momentum, left_factor, right_factor):
    slots, size, _ = momentum.shape
    owners, _, rows, _ = grad.shape
    shape = momentum.shape
    return call(
        state_kernel,
        "rest_of_state",
        (load,),
        [(grad, pl.ANY)]
        + [(array, pltpu.HBM) for array in (momentum, left_factor, right_factor)],
        [(shape, F32, pltpu.HBM), (shape, BF16, pltpu.HBM), (shape, BF16, pltpu.HBM)],
        [
            pltpu.VMEM((slots, owners, rows, size), BF16),
            pltpu.VMEM(shape, F32),
            pltpu.VMEM(shape, BF16),
            pltpu.VMEM(shape, BF16),
            DMA((slots, 4)),
            DMA((slots, 3)),
        ],
        4 * slots * size**3,
        18 * slots * size**2,
    )


def exchange(slabs):
    return lax.all_to_all(slabs, "shard", split_axis=0, concat_axis=0, tiled=True)


def body(
    grads, owner_table, momentum, variance, left_factor, right_factor, left_basis, right_basis
):
    owner_count = lax.axis_size("shard")
    capacity = momentum.shape[0]
    local = grads[0]
    _, rows, width = local.shape
    up = lambda x: lax.ppermute(x, "dp", [(i, (i + 1) % REPLICAS) for i in range(REPLICAS)])
    down = lambda x: lax.ppermute(x, "dp", [((i + 1) % REPLICAS, i) for i in range(REPLICAS)])

    relay_up, relay_down = copy_halves(local, ((2, 0), (2, 1)), "copy_relayed")
    relay_up, relay_down = up(relay_up), down(relay_down)
    near_up, near_down, own_up, own_down, own_a, own_b = copy_halves(
        local, ((1, 1), (3, 0), (1, 0), (3, 1), (0, 0), (0, 1)), "copy_rest"
    )
    near_up, near_down = up(near_up), down(near_down)
    ahead = add_relayed(own_up, relay_up, "add_up")
    behind = add_relayed(own_down, relay_down, "add_down")
    table = owner_table[:, :, 0]
    ahead, behind, table = lax.optimization_barrier((ahead, behind, table))
    ahead, behind = up(ahead), down(behind)
    place, load, *prepared = turn_moment(
        table, owner_count, momentum, variance, left_basis, right_basis
    )

    outgoing = sum_and_place(
        (own_a, own_b), (ahead, near_down), (near_up, behind), place, owner_count * capacity
    ).reshape(owner_count, capacity, rows, width)
    grad = exchange(outgoing)
    new_variance, update = owner_step(load, grad, *prepared)
    returned = exchange(update)
    new_momentum, new_left, new_right = rest_of_state(
        load, grad, momentum, left_factor, right_factor
    )
    update_rows = take_blocks(returned.reshape(owner_count * capacity, rows, width), place)
    return (update_rows, new_momentum, new_variance, new_left, new_right)


def solution(mesh):
    state = P(("dp", "shard"), None, None)
    return jax.shard_map(
        body,
        mesh=mesh,
        in_specs=(P("dp", None, "shard", None), P(), state, state, state, state, state, state),
        out_specs=(P("dp", "shard", None), state, state, state, state),
        check_vma=False,
    )
```

```python
import functools

import jax
import jax.numpy as jnp
from jax import lax
from jax.experimental import pallas as pl
from jax.experimental.pallas import tpu as pltpu
from jax.sharding import PartitionSpec as P

beta_moment = 0.95
beta_second = 0.95
beta_factor = 0.95
epsilon = 1e-08

F32 = jnp.float32
BF16 = jnp.bfloat16
VMEM_LIMIT = 32 * 1024 * 1024


def dot_nn(a, b):
    return lax.dot_general(a, b, (((1,), (0,)), ((), ())), preferred_element_type=F32)


def dot_tn(a, b):
    return lax.dot_general(a, b, (((0,), (0,)), ((), ())), preferred_element_type=F32)


def dot_nt(a, b):
    return lax.dot_general(a, b, (((1,), (1,)), ((), ())), preferred_element_type=F32)


ANYWHERE = pl.BlockSpec(memory_space=pl.ANY)
IN_VMEM = pl.BlockSpec(memory_space=pltpu.VMEM)
IN_SMEM = pl.BlockSpec(memory_space=pltpu.SMEM)
DMA = pltpu.SemaphoreType.DMA
REPLICAS = 4
CUTS = 2


def call(kernel, name, scalars, operands, outs, scratch, flops, accessed):
    def place(array, where):
        free = where in (pl.ANY, pltpu.SMEM)
        return array if free else pltpu.with_memory_space_constraint(array, where)

    spaces = [where for _, where in operands]
    spec = lambda where: {pltpu.VMEM: IN_VMEM, pltpu.SMEM: IN_SMEM}.get(where, ANYWHERE)
    return pl.pallas_call(
        kernel,
        out_shape=[
            jax.ShapeDtypeStruct(shape, dtype) if where is pl.ANY else where(shape, dtype)
            for shape, dtype, where in outs
        ],
        grid_spec=pltpu.PrefetchScalarGridSpec(
            num_scalar_prefetch=len(scalars),
            grid=(1,),
            in_specs=[spec(where) for where in spaces],
            out_specs=[spec(where) for _, _, where in outs],
            scratch_shapes=scratch,
        ),
        compiler_params=pltpu.CompilerParams(vmem_limit_bytes=VMEM_LIMIT),
        cost_estimate=pl.CostEstimate(flops=flops, bytes_accessed=accessed, transcendentals=0),
        name=name,
    )(*scalars, *[place(array, where) for array, where in operands])


def ahead_of(group, hops):
    return lax.rem(group + hops, REPLICAS)


def copy_kernel(halves, local_ref, *refs):
    outs, sem = refs[:-1], refs[-1]
    group = lax.axis_index("dp")
    count = outs[0].shape[0]
    step = count // CUTS
    reads = []
    for k, (hops, half) in enumerate(halves):
        first = (2 * ahead_of(group, hops) + half) * count
        for i in range(CUTS):
            reads.append(
                pltpu.make_async_copy(
                    local_ref.at[pl.ds(first + i * step, step)],
                    outs[k].at[pl.ds(i * step, step)],
                    sem.at[k, i],
                )
            )
            reads[-1].start()
    for read in reads:
        read.wait()


def copy_halves(local, halves, name):
    blocks, rows, width = local.shape
    count = blocks // REPLICAS // 2
    return call(
        functools.partial(copy_kernel, halves),
        name,
        (),
        [(local, pltpu.HBM)],
        [((count, rows, width), BF16, pltpu.VMEM)] * len(halves),
        [DMA((len(halves), CUTS))],
        0,
        2 * len(halves) * count * rows * width,
    )


def add_kernel(own_ref, got_ref, out_ref):
    def step(j, carry):
        out_ref[j] = (own_ref[j].astype(F32) + got_ref[j].astype(F32)).astype(BF16)
        return carry

    lax.fori_loop(0, own_ref.shape[0], step, 0, unroll=4)


def add_relayed(own, got, name):
    return call(
        add_kernel,
        name,
        (),
        [(own, pltpu.VMEM), (got, pltpu.VMEM)],
        [(own.shape, BF16, pltpu.VMEM)],
        [],
        own.size,
        6 * own.size,
    )[0]


def place_kernel(place_ref, own_a, own_b, a1, a2, b1, b2, out_ref):
    count = a1.shape[0]
    for own, left, right, base in ((own_a, a1, a2, 0), (own_b, b1, b2, count)):

        def step(j, carry, own=own, left=left, right=right, base=base):
            total = own[j].astype(F32) + (left[j].astype(F32) + right[j].astype(F32))
            out_ref[place_ref[base + j]] = total.astype(BF16)
            return carry

        lax.fori_loop(0, count, step, 0, unroll=4)


def sum_and_place(own, a, b, place, slots):
    count, rows, width = a[0].shape
    return call(
        place_kernel,
        "sum_and_place",
        (place,),
        [(array, pltpu.VMEM) for array in (*own, *a, *b)],
        [((slots, rows, width), BF16, pltpu.VMEM)],
        [],
        4 * count * rows * width,
        16 * count * rows * width,
    )[0]


def take_kernel(place_ref, source_ref, out_ref, sem):
    def step(j, carry):
        pltpu.make_async_copy(source_ref.at[place_ref[j]], out_ref.at[j], sem).start()
        return carry

    lax.fori_loop(0, out_ref.shape[0], step, 0, unroll=4)
    pltpu.make_async_copy(out_ref, out_ref, sem).wait()


def take_blocks(source, place):
    _, rows, width = source.shape
    count = place.shape[0]
    return call(
        take_kernel,
        "take_blocks",
        (place,),
        [(source, pltpu.VMEM)],
        [((count, rows, width), BF16, pltpu.HBM)],
        [DMA(())],
        0,
        4 * count * rows * width,
    )[0]


def turn_kernel(
    table_ref,
    mom_ref,
    var_ref,
    left_ref,
    right_ref,
    place_out,
    load_out,
    turned,
    var,
    left,
    right,
    mom,
    counts,
    into,
):
    slots = mom.shape[0]
    pairs = ((mom_ref, mom), (left_ref, left), (right_ref, right), (var_ref, var))
    reads = [
        [pltpu.make_async_copy(a.at[s], b.at[s], into.at[s, k]) for k, (a, b) in enumerate(pairs)]
        for s in range(slots)
    ]
    for row in reads:
        for read in row:
            read.start()

    owner_count = counts.shape[0]
    group, own_index = lax.axis_index("dp"), lax.axis_index("shard")

    def clear(i, carry):
        counts[i] = 0
        return carry

    def rank(j, carry):
        owner = table_ref[group, j]
        seen = counts[owner]
        counts[owner] = seen + 1
        place_out[j] = owner * slots + seen
        return carry

    lax.fori_loop(0, owner_count, clear, 0)
    lax.fori_loop(0, place_out.shape[0], rank, 0)
    load_out[0] = counts[own_index]

    for s in range(slots):
        for read in reads[s]:
            read.wait()
        half = (beta_moment * mom[s]).astype(BF16)
        turned[s] = dot_nn(dot_tn(left[s], half).astype(BF16), right[s])


def turn_moment(table, owner_count, momentum, variance, left_basis, right_basis):
    slots, size, _ = momentum.shape
    shape = momentum.shape
    return call(
        turn_kernel,
        "turn_moment",
        (),
        [(table, pltpu.SMEM)]
        + [(array, pltpu.HBM) for array in (momentum, variance, left_basis, right_basis)],
        [
            ((table.shape[1],), jnp.int32, pltpu.SMEM),
            ((1,), jnp.int32, pltpu.SMEM),
            (shape, F32, pltpu.VMEM),
            (shape, F32, pltpu.VMEM),
            (shape, BF16, pltpu.VMEM),
            (shape, BF16, pltpu.VMEM),
        ],
        [
            pltpu.VMEM(shape, F32),
            pltpu.SMEM((owner_count,), jnp.int32),
            DMA((slots, 4)),
        ],
        4 * slots * size**3,
        12 * slots * size**2,
    )


def step_kernel(
    grad, turned, var, left, right, upd_out, upd, out_of
):
    slots, size, _ = var.shape
    writes = [
        pltpu.make_async_copy(upd.at[s], upd_out.at[:, s], out_of.at[s]) for s in range(slots)
    ]

    def rotate(s):
        block = grad[:, s].reshape(size, size)
        return dot_nn(dot_tn(left[s], block).astype(BF16), right[s])

    def finish(s, rotated):
        second = beta_second * var[s] + (1.0 - beta_second) * rotated * rotated
        rotated_moment = turned[s] + (1.0 - beta_moment) * rotated
        direction = (rotated_moment / (jnp.sqrt(second) + epsilon)).astype(BF16)
        back_half = dot_nn(left[s], direction).astype(BF16)
        update = dot_nt(back_half, right[s]).astype(BF16)
        upd[s] = update.reshape(upd.shape[1:])
        writes[s].start()

    rotated = rotate(0)
    for s in range(slots):
        ahead = rotate(s + 1) if s + 1 < slots else None
        finish(s, rotated)
        rotated = ahead
    for write in writes:
        write.wait()


def owner_step(grad, turned, variance, left_basis, right_basis):
    slots, size, _ = variance.shape
    owners, _, rows, _ = grad.shape
    slabs = pltpu.VMEM((slots, owners, rows, size), BF16)
    return call(
        step_kernel,
        "owner_step",
        (),
        [(array, pltpu.VMEM) for array in (grad, turned, variance, left_basis, right_basis)],
        [(grad.shape, BF16, pltpu.HBM)],
        [slabs, DMA((slots,))],
        8 * slots * size**3,
        8 * slots * size**2,
    )[0]


def state_kernel(
    load_ref,
    grad_ref,
    mom_ref,
    left_ref,
    right_ref,
    var_ref,
    left_basis_ref,
    right_basis_ref,
    mom_out,
    left_out,
    right_out,
    var_out,
    grad,
    mom,
    left,
    right,
    var,
    left_basis,
    right_basis,
    into,
    out_of,
):
    slots, size, _ = mom.shape
    pairs = (
        (mom_ref, mom),
        (left_ref, left),
        (right_ref, right),
        (var_ref, var),
        (left_basis_ref, left_basis),
        (right_basis_ref, right_basis),
    )
    reads = [
        [pltpu.make_async_copy(grad_ref.at[:, s], grad.at[s], into.at[s, len(pairs)])]
        + [pltpu.make_async_copy(a.at[s], b.at[s], into.at[s, k]) for k, (a, b) in enumerate(pairs)]
        for s in range(slots)
    ]
    pairs = ((mom, mom_out), (left, left_out), (right, right_out), (var, var_out))
    writes = [
        [pltpu.make_async_copy(a.at[s], b.at[s], out_of.at[s, k]) for k, (a, b) in enumerate(pairs)]
        for s in range(slots)
    ]
    for row in reads:
        for read in row:
            read.start()
    for s in range(slots):
        for read in reads[s]:
            read.wait()

        @pl.when(s < load_ref[0])
        def _():
            block = grad[s].reshape(size, size)
            mom[s] = beta_moment * mom[s] + (1.0 - beta_moment) * block.astype(F32)
            outer = dot_nt(block, block)
            left[s] = (beta_factor * left[s].astype(F32) + (1.0 - beta_factor) * outer).astype(BF16)
            outer = dot_tn(block, block)
            right[s] = (beta_factor * right[s].astype(F32) + (1.0 - beta_factor) * outer).astype(
                BF16
            )
            rotated = dot_nn(dot_tn(left_basis[s], block).astype(BF16), right_basis[s])
            var[s] = beta_second * var[s] + (1.0 - beta_second) * rotated * rotated

        for write in writes[s]:
            write.start()
    for row in writes:
        for write in row:
            write.wait()


def rest_of_state(load, grad, *state):
    momentum = state[0]
    slots, size, _ = momentum.shape
    owners, _, rows, _ = grad.shape
    shape = momentum.shape
    return call(
        state_kernel,
        "rest_of_state",
        (load,),
        [(grad, pl.ANY)] + [(array, pltpu.HBM) for array in state],
        [(shape, dtype, pltpu.HBM) for dtype in (F32, BF16, BF16, F32)],
        [
            pltpu.VMEM((slots, owners, rows, size), BF16),
            pltpu.VMEM(shape, F32),
            pltpu.VMEM(shape, BF16),
            pltpu.VMEM(shape, BF16),
            pltpu.VMEM(shape, F32),
            pltpu.VMEM(shape, BF16),
            pltpu.VMEM(shape, BF16),
            DMA((slots, 7)),
            DMA((slots, 4)),
        ],
        8 * slots * size**3,
        18 * slots * size**2,
    )


def exchange(slabs):
    return lax.all_to_all(slabs, "shard", split_axis=0, concat_axis=0, tiled=True)


def body(
    grads, owner_table, momentum, variance, left_factor, right_factor, left_basis, right_basis
):
    owner_count = lax.axis_size("shard")
    capacity = momentum.shape[0]
    local = grads[0]
    _, rows, width = local.shape
    up = lambda x: lax.ppermute(x, "dp", [(i, (i + 1) % REPLICAS) for i in range(REPLICAS)])
    down = lambda x: lax.ppermute(x, "dp", [((i + 1) % REPLICAS, i) for i in range(REPLICAS)])

    relay_up, relay_down = copy_halves(local, ((2, 0), (2, 1)), "copy_relayed")
    relay_up, relay_down = up(relay_up), down(relay_down)
    near_up, near_down, own_up, own_down, own_a, own_b = copy_halves(
        local, ((1, 1), (3, 0), (1, 0), (3, 1), (0, 0), (0, 1)), "copy_rest"
    )
    near_up, near_down = up(near_up), down(near_down)
    ahead = add_relayed(own_up, relay_up, "add_up")
    behind = add_relayed(own_down, relay_down, "add_down")
    table = owner_table[:, :, 0]
    ahead, behind, table = lax.optimization_barrier((ahead, behind, table))
    ahead, behind = up(ahead), down(behind)
    place, load, *prepared = turn_moment(
        table, owner_count, momentum, variance, left_basis, right_basis
    )

    outgoing = sum_and_place(
        (own_a, own_b), (ahead, near_down), (near_up, behind), place, owner_count * capacity
    ).reshape(owner_count, capacity, rows, width)
    grad = exchange(outgoing)
    update = owner_step(grad, *prepared)
    returned = exchange(update)
    new_momentum, new_left, new_right, new_variance = rest_of_state(
        load, grad, momentum, left_factor, right_factor, variance, left_basis, right_basis
    )
    update_rows = take_blocks(returned.reshape(owner_count * capacity, rows, width), place)
    return (update_rows, new_momentum, new_variance, new_left, new_right)


def solution(mesh):
    state = P(("dp", "shard"), None, None)
    return jax.shard_map(
        body,
        mesh=mesh,
        in_specs=(P("dp", None, "shard", None), P(), state, state, state, state, state, state),
        out_specs=(P("dp", "shard", None), state, state, state, state),
        check_vma=False,
    )
```

```python
import functools

import jax
import jax.numpy as jnp
from jax import lax
from jax.experimental import pallas as pl
from jax.experimental.pallas import tpu as pltpu
from jax.sharding import PartitionSpec as P

beta_moment = 0.95
beta_second = 0.95
beta_factor = 0.95
epsilon = 1e-08

F32 = jnp.float32
BF16 = jnp.bfloat16
VMEM_LIMIT = 32 * 1024 * 1024


def dot_nn(a, b):
    return lax.dot_general(a, b, (((1,), (0,)), ((), ())), preferred_element_type=F32)


def dot_tn(a, b):
    return lax.dot_general(a, b, (((0,), (0,)), ((), ())), preferred_element_type=F32)


def dot_nt(a, b):
    return lax.dot_general(a, b, (((1,), (1,)), ((), ())), preferred_element_type=F32)


ANYWHERE = pl.BlockSpec(memory_space=pl.ANY)
IN_VMEM = pl.BlockSpec(memory_space=pltpu.VMEM)
IN_SMEM = pl.BlockSpec(memory_space=pltpu.SMEM)
DMA = pltpu.SemaphoreType.DMA
REPLICAS = 4
CUTS = 2


def call(kernel, name, scalars, operands, outs, scratch, flops, accessed):
    def place(array, where):
        free = where in (pl.ANY, pltpu.SMEM)
        return array if free else pltpu.with_memory_space_constraint(array, where)

    spaces = [where for _, where in operands]
    spec = lambda where: {pltpu.VMEM: IN_VMEM, pltpu.SMEM: IN_SMEM}.get(where, ANYWHERE)
    return pl.pallas_call(
        kernel,
        out_shape=[
            jax.ShapeDtypeStruct(shape, dtype) if where is pl.ANY else where(shape, dtype)
            for shape, dtype, where in outs
        ],
        grid_spec=pltpu.PrefetchScalarGridSpec(
            num_scalar_prefetch=len(scalars),
            grid=(1,),
            in_specs=[spec(where) for where in spaces],
            out_specs=[spec(where) for _, _, where in outs],
            scratch_shapes=scratch,
        ),
        compiler_params=pltpu.CompilerParams(vmem_limit_bytes=VMEM_LIMIT),
        cost_estimate=pl.CostEstimate(flops=flops, bytes_accessed=accessed, transcendentals=0),
        name=name,
    )(*scalars, *[place(array, where) for array, where in operands])


def ahead_of(group, hops):
    return lax.rem(group + hops, REPLICAS)


def copy_kernel(halves, local_ref, *refs):
    outs, sem = refs[:-1], refs[-1]
    group = lax.axis_index("dp")
    count = outs[0].shape[0]
    step = count // CUTS
    reads = []
    for k, (hops, half) in enumerate(halves):
        first = (2 * ahead_of(group, hops) + half) * count
        for i in range(CUTS):
            reads.append(
                pltpu.make_async_copy(
                    local_ref.at[pl.ds(first + i * step, step)],
                    outs[k].at[pl.ds(i * step, step)],
                    sem.at[k, i],
                )
            )
            reads[-1].start()
    for read in reads:
        read.wait()


def copy_halves(local, halves, name):
    blocks, rows, width = local.shape
    count = blocks // REPLICAS // 2
    return call(
        functools.partial(copy_kernel, halves),
        name,
        (),
        [(local, pltpu.HBM)],
        [((count, rows, width), BF16, pltpu.VMEM)] * len(halves),
        [DMA((len(halves), CUTS))],
        0,
        2 * len(halves) * count * rows * width,
    )


def add_kernel(own_ref, got_ref, out_ref):
    def step(j, carry):
        out_ref[j] = (own_ref[j].astype(F32) + got_ref[j].astype(F32)).astype(BF16)
        return carry

    lax.fori_loop(0, own_ref.shape[0], step, 0, unroll=4)


def add_relayed(own, got, name):
    return call(
        add_kernel,
        name,
        (),
        [(own, pltpu.VMEM), (got, pltpu.VMEM)],
        [(own.shape, BF16, pltpu.VMEM)],
        [],
        own.size,
        6 * own.size,
    )[0]


def place_kernel(place_ref, own_a, own_b, a1, a2, b1, b2, out_ref):
    count = a1.shape[0]
    for own, left, right, base in ((own_a, a1, a2, 0), (own_b, b1, b2, count)):

        def step(j, carry, own=own, left=left, right=right, base=base):
            total = own[j].astype(F32) + (left[j].astype(F32) + right[j].astype(F32))
            out_ref[place_ref[base + j]] = total.astype(BF16)
            return carry

        lax.fori_loop(0, count, step, 0, unroll=4)


def sum_and_place(own, a, b, place, slots):
    count, rows, width = a[0].shape
    return call(
        place_kernel,
        "sum_and_place",
        (place,),
        [(array, pltpu.VMEM) for array in (*own, *a, *b)],
        [((slots, rows, width), BF16, pltpu.VMEM)],
        [],
        4 * count * rows * width,
        16 * count * rows * width,
    )[0]


def take_kernel(place_ref, source_ref, out_ref, sem):
    def step(j, carry):
        pltpu.make_async_copy(source_ref.at[place_ref[j]], out_ref.at[j], sem).start()
        return carry

    lax.fori_loop(0, out_ref.shape[0], step, 0, unroll=4)
    pltpu.make_async_copy(out_ref, out_ref, sem).wait()


def take_blocks(source, place):
    _, rows, width = source.shape
    count = place.shape[0]
    return call(
        take_kernel,
        "take_blocks",
        (place,),
        [(source, pltpu.VMEM)],
        [((count, rows, width), BF16, pltpu.HBM)],
        [DMA(())],
        0,
        4 * count * rows * width,
    )[0]


def turn_kernel(
    table_ref,
    mom_ref,
    var_ref,
    left_ref,
    right_ref,
    place_out,
    load_out,
    turned,
    var,
    left,
    right,
    mom,
    counts,
    into,
):
    slots = mom.shape[0]
    pairs = ((mom_ref, mom), (left_ref, left), (right_ref, right), (var_ref, var))
    reads = [
        [pltpu.make_async_copy(a.at[s], b.at[s], into.at[s, k]) for k, (a, b) in enumerate(pairs)]
        for s in range(slots)
    ]
    for row in reads:
        for read in row:
            read.start()

    owner_count = counts.shape[0]
    group, own_index = lax.axis_index("dp"), lax.axis_index("shard")

    def clear(i, carry):
        counts[i] = 0
        return carry

    def rank(j, carry):
        owner = table_ref[group, j]
        seen = counts[owner]
        counts[owner] = seen + 1
        place_out[j] = owner * slots + seen
        return carry

    lax.fori_loop(0, owner_count, clear, 0)
    lax.fori_loop(0, place_out.shape[0], rank, 0)
    load_out[0] = counts[own_index]

    for s in range(slots):
        for read in reads[s]:
            read.wait()
        half = (beta_moment * mom[s]).astype(BF16)
        turned[s] = dot_nn(dot_tn(left[s], half).astype(BF16), right[s])


def turn_moment(table, owner_count, momentum, variance, left_basis, right_basis):
    slots, size, _ = momentum.shape
    shape = momentum.shape
    return call(
        turn_kernel,
        "turn_moment",
        (),
        [(table, pltpu.SMEM)]
        + [(array, pltpu.HBM) for array in (momentum, variance, left_basis, right_basis)],
        [
            ((table.shape[1],), jnp.int32, pltpu.SMEM),
            ((1,), jnp.int32, pltpu.SMEM),
            (shape, F32, pltpu.VMEM),
            (shape, F32, pltpu.VMEM),
            (shape, BF16, pltpu.VMEM),
            (shape, BF16, pltpu.VMEM),
        ],
        [
            pltpu.VMEM(shape, F32),
            pltpu.SMEM((owner_count,), jnp.int32),
            DMA((slots, 4)),
        ],
        4 * slots * size**3,
        12 * slots * size**2,
    )


def step_kernel(
    grad, turned, var, left, right, upd_out, upd, out_of
):
    slots, size, _ = var.shape
    writes = [
        pltpu.make_async_copy(upd.at[s], upd_out.at[:, s], out_of.at[s]) for s in range(slots)
    ]

    def rotate(s):
        block = grad[:, s].reshape(size, size)
        return dot_nn(dot_tn(left[s], block).astype(BF16), right[s])

    def finish(s, rotated):
        second = beta_second * var[s] + (1.0 - beta_second) * rotated * rotated
        rotated_moment = turned[s] + (1.0 - beta_moment) * rotated
        direction = (rotated_moment / (second * lax.rsqrt(second) + epsilon)).astype(BF16)
        back_half = dot_nn(left[s], direction).astype(BF16)
        update = dot_nt(back_half, right[s]).astype(BF16)
        upd[s] = update.reshape(upd.shape[1:])
        writes[s].start()

    rotated = rotate(0)
    for s in range(slots):
        ahead = rotate(s + 1) if s + 1 < slots else None
        finish(s, rotated)
        rotated = ahead
    for write in writes:
        write.wait()


def owner_step(grad, turned, variance, left_basis, right_basis):
    slots, size, _ = variance.shape
    owners, _, rows, _ = grad.shape
    slabs = pltpu.VMEM((slots, owners, rows, size), BF16)
    return call(
        step_kernel,
        "owner_step",
        (),
        [(array, pltpu.VMEM) for array in (grad, turned, variance, left_basis, right_basis)],
        [(grad.shape, BF16, pltpu.HBM)],
        [slabs, DMA((slots,))],
        8 * slots * size**3,
        8 * slots * size**2,
    )[0]


def state_kernel(
    load_ref,
    grad_ref,
    mom_ref,
    left_ref,
    right_ref,
    var_ref,
    left_basis_ref,
    right_basis_ref,
    mom_out,
    left_out,
    right_out,
    var_out,
    grad,
    mom,
    left,
    right,
    var,
    left_basis,
    right_basis,
    into,
    out_of,
):
    slots, size, _ = mom.shape
    pairs = (
        (mom_ref, mom),
        (left_ref, left),
        (right_ref, right),
        (var_ref, var),
        (left_basis_ref, left_basis),
        (right_basis_ref, right_basis),
    )
    reads = [
        [pltpu.make_async_copy(grad_ref.at[:, s], grad.at[s], into.at[s, len(pairs)])]
        + [pltpu.make_async_copy(a.at[s], b.at[s], into.at[s, k]) for k, (a, b) in enumerate(pairs)]
        for s in range(slots)
    ]
    pairs = ((mom, mom_out), (left, left_out), (right, right_out), (var, var_out))
    writes = [
        [pltpu.make_async_copy(a.at[s], b.at[s], out_of.at[s, k]) for k, (a, b) in enumerate(pairs)]
        for s in range(slots)
    ]
    for row in reads:
        for read in row:
            read.start()
    for s in range(slots):
        for read in reads[s]:
            read.wait()

        @pl.when(s < load_ref[0])
        def _():
            block = grad[s].reshape(size, size)
            mom[s] = beta_moment * mom[s] + (1.0 - beta_moment) * block.astype(F32)
            outer = dot_nt(block, block)
            left[s] = (beta_factor * left[s].astype(F32) + (1.0 - beta_factor) * outer).astype(BF16)
            outer = dot_tn(block, block)
            right[s] = (beta_factor * right[s].astype(F32) + (1.0 - beta_factor) * outer).astype(
                BF16
            )
            rotated = dot_nn(dot_tn(left_basis[s], block).astype(BF16), right_basis[s])
            var[s] = beta_second * var[s] + (1.0 - beta_second) * rotated * rotated

        for write in writes[s]:
            write.start()
    for row in writes:
        for write in row:
            write.wait()


def rest_of_state(load, grad, *state):
    momentum = state[0]
    slots, size, _ = momentum.shape
    owners, _, rows, _ = grad.shape
    shape = momentum.shape
    return call(
        state_kernel,
        "rest_of_state",
        (load,),
        [(grad, pl.ANY)] + [(array, pltpu.HBM) for array in state],
        [(shape, dtype, pltpu.HBM) for dtype in (F32, BF16, BF16, F32)],
        [
            pltpu.VMEM((slots, owners, rows, size), BF16),
            pltpu.VMEM(shape, F32),
            pltpu.VMEM(shape, BF16),
            pltpu.VMEM(shape, BF16),
            pltpu.VMEM(shape, F32),
            pltpu.VMEM(shape, BF16),
            pltpu.VMEM(shape, BF16),
            DMA((slots, 7)),
            DMA((slots, 4)),
        ],
        8 * slots * size**3,
        18 * slots * size**2,
    )


def exchange(slabs):
    return lax.all_to_all(slabs, "shard", split_axis=0, concat_axis=0, tiled=True)


def body(
    grads, owner_table, momentum, variance, left_factor, right_factor, left_basis, right_basis
):
    owner_count = lax.axis_size("shard")
    capacity = momentum.shape[0]
    local = grads[0]
    _, rows, width = local.shape
    down = lambda x: lax.ppermute(x, "dp", [(i, (i + 1) % REPLICAS) for i in range(REPLICAS)])
    up = lambda x: lax.ppermute(x, "dp", [((i + 1) % REPLICAS, i) for i in range(REPLICAS)])

    relay_up, relay_down = copy_halves(local, ((2, 0), (2, 1)), "copy_relayed")
    relay_up, relay_down = up(relay_up), down(relay_down)
    near_up, near_down, own_up, own_down, own_a, own_b = copy_halves(
        local, ((3, 1), (1, 0), (3, 0), (1, 1), (0, 0), (0, 1)), "copy_rest"
    )
    near_up, near_down = up(near_up), down(near_down)
    ahead = add_relayed(own_up, relay_up, "add_up")
    behind = add_relayed(own_down, relay_down, "add_down")
    table = owner_table[:, :, 0]
    ahead = up(ahead)
    behind, table = lax.optimization_barrier((behind, table))
    behind = down(behind)
    place, load, *prepared = turn_moment(
        table, owner_count, momentum, variance, left_basis, right_basis
    )

    outgoing = sum_and_place(
        (own_a, own_b), (ahead, near_down), (near_up, behind), place, owner_count * capacity
    ).reshape(owner_count, capacity, rows, width)
    grad = exchange(outgoing)
    update = owner_step(grad, *prepared)
    returned = exchange(update)
    new_momentum, new_left, new_right, new_variance = rest_of_state(
        load, grad, momentum, left_factor, right_factor, variance, left_basis, right_basis
    )
    update_rows = take_blocks(returned.reshape(owner_count * capacity, rows, width), place)
    return (update_rows, new_momentum, new_variance, new_left, new_right)


def solution(mesh):
    state = P(("dp", "shard"), None, None)
    return jax.shard_map(
        body,
        mesh=mesh,
        in_specs=(P("dp", None, "shard", None), P(), state, state, state, state, state, state),
        out_specs=(P("dp", "shard", None), state, state, state, state),
        check_vma=False,
    )
```
